32 devices in a mesh: grp: 4 (over y, x), dev: 8 (over z, core).
Axes of the slice: x: 2, y: 2, z: 4, core: 2. Of those that a mesh axis runs over, the one named last changes fastest.
Arguments:
- state: float32 [2, 8, 131072], P(None, None, ('grp', 'dev')), may hold values from -6 to 6
- gates: float32 [2, 4, 2, 128, 128], replicated, may hold values from -0.375 to 0.375
- local_perm: int32 [2, 12], replicated, may hold values from 0 to 11, each once within a row
Outputs:
- final_state: float32 [2, 8, 131072], P(None, None, ('grp', 'dev'))
The draws below stay inside these ranges and needn't reach their ends.
Inputs may be any that keep to these rules, and one draw needn't show every extreme that they name: Each row of local_perm names each of the 12 local qubits once.
All inputs are finite; a program needn't handle non-finite values.
Results may differ from the reference program's by a relative error of at most 0.0001.
Values sent between devices are 32-bit elements; how exact they have to be, the bound alone decides.
A program may use at most 64 MiB of HBM per device.

```python
import jax
import jax.numpy as jnp
from jax import lax

GATE_DIM = 128
LOCAL_QUBITS = 12
TRAJ = 8
CYCLES = 2
AMPS = 131072
N_GRP = 4
N_DEV = 8


def shard_levels(stream_key, shape, shards, least, high):
    def one(position, shards_of):
        heights = jax.random.uniform(jax.random.fold_in(jax.random.fold_in(stream_key, 6), position), (shards_of,), jnp.float32, least / len(shards), high / len(shards))
        return jnp.repeat(jnp.exp(heights), shape[position] // shards_of).reshape((-1,) + (1,) * (len(shape) - position - 1))

    factor_of = one(*shards[0])
    for cut in shards[1:]:
        factor_of = factor_of * one(*cut)
    return factor_of


def bell_draw(rng, dims, spread, reach, shards=(), kind=jnp.bfloat16):
    entries = spread * jax.random.normal(rng, dims, jnp.float32)
    if shards:
        entries = entries * shard_levels(rng, dims, shards, -0.22, 0.18)
    return jnp.clip(entries, -reach, reach).astype(kind)


def setup_inputs(seed: int = 0) -> dict:
    streams_of = jax.random.split(jax.random.key(seed), 4)
    return {
        "state": bell_draw(streams_of[0], (2, TRAJ, AMPS), 1.0, 6.0, ((2, 32),), jnp.float32),
        "gates": bell_draw(streams_of[1], (CYCLES, 4, 2, GATE_DIM, GATE_DIM), (2 * GATE_DIM) ** -0.5, 0.375, (), jnp.float32),
        "local_perm": jax.vmap(lambda own: jax.random.permutation(own, LOCAL_QUBITS))(jax.random.split(streams_of[2], CYCLES)).reshape((CYCLES, LOCAL_QUBITS)).astype(jnp.int32),
    }


def source_index(perm_row, nbits):
    positions = jnp.arange(2 ** nbits, dtype=jnp.int32)
    shifts = jnp.arange(nbits, dtype=jnp.int32)
    bits = (positions[:, None] >> shifts[None, :]) & 1
    return jnp.sum(bits << perm_row.astype(jnp.int32)[None, :], axis=1).astype(jnp.int32)


def complex_apply(real_part, imag_part, gate, form):
    high = lax.Precision.HIGHEST
    gate_re = gate[0]
    gate_im = gate[1]
    out_re = jnp.einsum(form, real_part, gate_re, precision=high) - jnp.einsum(form, imag_part, gate_im, precision=high)
    out_im = jnp.einsum(form, real_part, gate_im, precision=high) + jnp.einsum(form, imag_part, gate_re, precision=high)
    return jnp.stack([out_re, out_im])


def gate_low(amps, gate):
    shape = amps.shape
    blocks = amps.reshape(2, shape[1], -1, GATE_DIM)
    return complex_apply(blocks[0], blocks[1], gate, "bmk,ik->bmi").reshape(shape)


def gate_high(amps, gate):
    shape = amps.shape
    blocks = amps.reshape(2, shape[1], shape[2], GATE_DIM, -1)
    return complex_apply(blocks[0], blocks[1], gate, "bgkm,ik->bgim").reshape(shape)


def reference(state, gates, local_perm):
    grp_bits = N_GRP.bit_length() - 1
    dev_amps = 2 ** LOCAL_QUBITS
    amps = state.reshape(2, TRAJ, N_GRP * N_DEV, dev_amps)
    for cycle in range(CYCLES):
        source = source_index(local_perm[cycle], LOCAL_QUBITS)
        amps = jnp.take(amps, source, axis=3)
        amps = gate_low(amps, gates[cycle, 0])
        amps = gate_high(amps, gates[cycle, 1])
        which = cycle % grp_bits
        split = amps.reshape(2, TRAJ, N_GRP >> (which + 1), 2, 1 << which, N_DEV, 2, dev_amps // 2)
        amps = jnp.swapaxes(split, 3, 6).reshape(2, TRAJ, N_GRP * N_DEV, dev_amps)
        amps = gate_low(amps, gates[cycle, 2])
        split = amps.reshape(2, TRAJ, N_GRP, N_DEV, N_DEV, dev_amps // N_DEV)
        amps = jnp.swapaxes(split, 3, 4).reshape(2, TRAJ, N_GRP * N_DEV, dev_amps)
        amps = gate_high(amps, gates[cycle, 3])
    return amps.reshape(2, TRAJ, -1)
```

```python
import functools

import jax
import jax.numpy as jnp
from jax import lax
from jax.experimental import pallas as pl
from jax.experimental.pallas import tpu as pltpu
from jax.sharding import PartitionSpec as P

MESH = pl.DeviceIdType.MESH
CYCLES = 2


def bits_of(count, nbits):
    return jnp.arange(count, dtype=jnp.int32)[:, None] >> jnp.arange(nbits, dtype=jnp.int32)[None, :] & 1


def permutation_plan(perm, gate_bits):
    nbits = perm.shape[0]
    row_bits = nbits - gate_bits
    own = jnp.arange(nbits, dtype=jnp.int32)
    hit = perm[:, None] == own[None, :]
    inverse = jnp.sum(jnp.where(hit, own[:, None], 0), axis=0)
    leaves = inverse[:gate_bits] >= gate_bits
    enters = inverse[gate_bits:] < gate_bits
    open_slot = jnp.concatenate([enters, jnp.zeros((gate_bits - row_bits,), bool)])
    lane = jnp.arange(gate_bits)
    before = lane[None, :] < lane[:, None]

    def rank(flag):
        return jnp.sum((flag[:, None] == flag[None, :]) & before, axis=1)

    match = (leaves[:, None] == open_slot[None, :]) & (rank(leaves)[:, None] == rank(open_slot)[None, :])
    slot = jnp.sum(jnp.where(match, own[None, :gate_bits], 0), axis=1)
    position = jnp.concatenate(
        [
            slot + jnp.where(leaves, gate_bits, 0),
            jnp.where(enters, own[:row_bits], own[gate_bits:]),
        ]
    )
    placed = jnp.sum(jnp.where(hit, position[None, :], 0), axis=1)
    bits = bits_of(1 << gate_bits, gate_bits)
    shared = gate_bits - row_bits
    high_place = jnp.concatenate([own[row_bits:gate_bits], placed[gate_bits:] - gate_bits])
    maps = [jnp.sum(bits << place[None, :], axis=1) for place in (slot, placed[:gate_bits], high_place)]
    conditions = jnp.broadcast_to(enters[:, None], (row_bits, 1 << gate_bits)).astype(jnp.int32)
    return jnp.concatenate([jnp.stack(maps), conditions])


def split(x):
    high = x.astype(jnp.bfloat16)
    low = (x - high.astype(jnp.float32)).astype(jnp.bfloat16)
    return high, low


def dot(a, b, contract):
    return lax.dot_general(a, b, (contract, ((), ())), preferred_element_type=jnp.float32)


NT = ((1,), (1,))
NN = ((1,), (0,))


def swap_lane_bit(first, second, bit, lane, condition=None):
    width = first.shape[-1]
    axis = first.ndim - 1
    up = (lane >> bit & 1) == 1
    down = ~up
    if condition is not None:
        up = up & condition
        down = down & condition
    new_first = jnp.where(up, pltpu.roll(second, 1 << bit, axis), first)
    new_second = jnp.where(down, pltpu.roll(first, width - (1 << bit), axis), second)
    return new_first, new_second


def one_hot(lane_map):
    width = lane_map.shape[-1]
    rows = lax.broadcasted_iota(jnp.int32, (width, width), 0)
    return jnp.where(rows == lane_map, 1.0, 0.0).astype(jnp.bfloat16)


def gate_matrix(real, imag, columns):
    width = real.shape[-1]
    re_high, re_low = split(real)
    im_high, im_low = split(imag)
    if columns is not None:
        stack = jnp.concatenate([re_high, re_low, im_high, im_low])
        moved = dot(stack, columns, NT).astype(jnp.bfloat16)
        re_high, re_low, im_high, im_low = [moved[i * width : (i + 1) * width] for i in range(4)]

    def whole(re, im):
        return jnp.concatenate(
            [jnp.concatenate([re, -im], axis=1), jnp.concatenate([im, re], axis=1)], axis=0
        )

    return whole(re_high, im_high), whole(re_low, im_low)


def kernel(sizes, state_ref, gates_ref, plan_ref, out_ref, work, sent, landed, send_sem, recv_sem):
    traj, nbits, gate_bits, grp_bits, dev_bits = sizes
    width = 1 << gate_bits
    row_bits = nbits - gate_bits
    shared = gate_bits - row_bits
    rows = 1 << row_bits
    blocks = 1 << dev_bits
    top = blocks // 2
    wide = dev_bits > row_bits
    grp = lax.axis_index("grp")
    dev = lax.axis_index("dev")
    grp_low = grp % 2
    grp_next = grp // 2 % 2
    grp_rest = grp // 4 * 4
    dev_top = dev // top
    dev_low = dev % top

    def targets(cycle, step):
        low = (dev_low ^ (step % top)) if step % top else dev_low
        high = 1 - grp_next if step // top else grp_next
        block = high * top + low
        if cycle == 0:
            return block, grp_rest + high * 2 + grp_low, grp_next * top + low, dev
        return block, grp_rest + high * 2 + grp_next, dev_top * top + low, grp_low * top + dev_low

    self_sent = [dev_top == grp_next, grp_low == grp_next]

    barrier = pltpu.get_barrier_semaphore()
    for step in range(blocks):
        low = (dev_low ^ (step % top)) if step % top else dev_low
        high = step // top
        source_high = 1 - dev_top if high else dev_top
        first = (grp_rest + dev_top * 2 + grp_low, source_high * top + low)
        source_low = 1 - grp_low if high else grp_low
        second = (grp_rest + grp_low * 2 + source_low, dev_top * top + low)

        def tell(device):
            pl.semaphore_signal(barrier, inc=1, device_id=device, device_id_type=MESH)

        if step:
            tell(first)
            tell(second)
        else:
            pl.when(dev_top != grp_next)(functools.partial(tell, first))
            pl.when(grp_low != grp_next)(functools.partial(tell, second))

    lane = lax.broadcasted_iota(jnp.int32, (1, width), 1)
    fixed = one_hot((lane % (1 << shared)) * rows + lane // (1 << shared))

    def low_matrix(cycle, which, lane_map):
        columns = None if lane_map is None else one_hot(lane_map)
        return gate_matrix(gates_ref[cycle, which, 0], gates_ref[cycle, which, 1], columns)

    def high_matrix(cycle, which, columns):
        parts = []
        for part in range(2):
            parts.append(
                jnp.concatenate(
                    [
                        gates_ref[cycle, which, part, pl.ds(a, rows, stride=1 << shared), :]
                        for a in range(1 << shared)
                    ]
                )
            )
        return gate_matrix(parts[0], parts[1], columns)

    def apply_low(x, matrix):
        high, low = split(jnp.concatenate([x[0], x[1]], axis=1))
        m_high, m_low = matrix
        y = dot(high, m_high, NT) + (dot(low, m_high, NT) + dot(high, m_low, NT))
        return y[:, :width], y[:, width:]

    def swap_traj(planes):
        planes = list(planes)
        for bit in range(shared):
            for t in range(len(planes)):
                if not t >> bit & 1:
                    o = t | 1 << bit
                    planes[t], planes[o] = swap_lane_bit(planes[t], planes[o], row_bits + bit, lane)
        return planes

    def apply_high(source, matrix, write):
        per = 1 << shared
        operand = []
        for part in range(2):
            planes = [source[part, pl.ds(t, rows, stride=traj), :] for t in range(traj)]
            planes = swap_traj(planes)
            operand.append(
                jnp.concatenate(
                    [jnp.concatenate(planes[g : g + per], axis=0) for g in range(0, traj, per)], axis=1
                )
            )
        high, low = split(jnp.concatenate(operand, axis=0))
        m_high, m_low = matrix
        y = dot(m_high, high, NN) + (dot(m_low, high, NN) + dot(m_high, low, NN))
        for part in range(2):
            planes = [
                y[part * width + a * rows : part * width + (a + 1) * rows, g * width : (g + 1) * width]
                for g in range(traj // per)
                for a in range(per)
            ]
            planes = swap_traj(planes)
            for t in range(traj):
                write[part, pl.ds(t, rows, stride=traj), :] = planes[t]

    def local_part(x, cycle, matrices):
        plan = plan_ref[cycle]
        lanes = one_hot(plan[0:1])
        conditions = [plan[3 + j : 4 + j] == 1 for j in range(row_bits)]
        moved = []
        for part in range(2):
            high, low = split(x[part])
            y = dot(high, lanes, NT) + dot(low, lanes, NT)
            tiles = [y[r * traj : (r + 1) * traj] for r in range(rows)]
            for j in range(row_bits):
                for r in range(rows):
                    if not r >> j & 1:
                        o = r | 1 << j
                        tiles[r], tiles[o] = swap_lane_bit(tiles[r], tiles[o], j, lane, conditions[j])
            moved.append(jnp.concatenate(tiles))
        y = apply_low(moved, matrices[0])
        work[0] = y[0]
        work[1] = y[1]
        apply_high(work, matrices[1], work)
        y = apply_low([work[0], work[1]], matrices[2])
        if wide:
            y = swap_lane_bit(y[0], y[1], gate_bits - 1, lane)
        sent[cycle, 0] = y[0]
        sent[cycle, 1] = y[1]

    def matrices_of(cycle):
        plan = plan_ref[cycle]
        return (
            low_matrix(cycle, 0, plan[1:2]),
            high_matrix(cycle, 1, one_hot(plan[2:3])),
            low_matrix(cycle, 2, None),
        )

    def view(ref, cycle, block):
        if wide:
            start = pl.multiple_of(block // 2 * traj, traj)
            return ref.at[cycle, pl.ds(block % 2, 1), pl.ds(start, traj), :]
        depth = rows * traj // blocks
        start = pl.multiple_of(block * depth, depth)
        return ref.at[cycle, :, pl.ds(start, depth), :]

    def remote(cycle, step):
        block, to_grp, to_dev, slot = targets(cycle, step)
        return pltpu.make_async_remote_copy(
            src_ref=view(sent, cycle, block),
            dst_ref=view(landed, cycle, slot),
            send_sem=send_sem.at[cycle, step],
            recv_sem=recv_sem.at[cycle, slot],
            device_id=(to_grp, to_dev),
            device_id_type=MESH,
        )

    def stay(cycle):
        block, _, _, slot = targets(cycle, 0)
        return pltpu.make_async_copy(
            view(sent, cycle, block), view(landed, cycle, slot), recv_sem.at[cycle, slot]
        )

    def start(cycle):
        for step in range(blocks - 1, 0, -1):
            remote(cycle, step).start()

        @pl.when(self_sent[cycle])
        def _():
            stay(cycle).start()

        @pl.when(jnp.logical_not(self_sent[cycle]))
        def _():
            remote(cycle, 0).start()

    def finish(cycle):
        for slot in range(blocks):
            pltpu.make_async_copy(
                view(landed, cycle, slot), view(landed, cycle, slot), recv_sem.at[cycle, slot]
            ).wait()

    def finish_sends(cycle):
        for step in range(1, blocks):
            remote(cycle, step).wait_send()

        @pl.when(jnp.logical_not(self_sent[cycle]))
        def _():
            remote(cycle, 0).wait_send()

    def unwiden(cycle):
        if wide:
            y = swap_lane_bit(landed[cycle, 0], landed[cycle, 1], gate_bits - 1, lane)
            landed[cycle, 0] = y[0]
            landed[cycle, 1] = y[1]

    x = [
        jnp.concatenate([state_ref[part, :, r * width : (r + 1) * width] for r in range(rows)])
        for part in range(2)
    ]
    local_part(x, 0, matrices_of(0))
    others = 2 * (blocks - 1) + jnp.where(self_sent[0], 0, 1) + jnp.where(self_sent[1], 0, 1)
    pl.semaphore_wait(barrier, others)
    start(0)
    last = high_matrix(0, 3, fixed)
    following = matrices_of(1)
    finish(0)
    unwiden(0)
    apply_high(landed.at[0], last, work)
    local_part([work[0], work[1]], 1, following)
    start(1)
    last = high_matrix(1, 3, fixed)
    finish(1)
    unwiden(1)
    apply_high(landed.at[1], last, work)
    for part in range(2):
        for r in range(rows):
            out_ref[part, :, r * width : (r + 1) * width] = work[part, r * traj : (r + 1) * traj, :]
    finish_sends(0)
    finish_sends(1)


def on_device(state, gates, local_perm):
    traj = state.shape[1]
    nbits = state.shape[2].bit_length() - 1
    gate_bits = gates.shape[-1].bit_length() - 1
    grp_bits = lax.axis_size("grp").bit_length() - 1
    dev_bits = lax.axis_size("dev").bit_length() - 1
    plan = jnp.stack([permutation_plan(local_perm[c], gate_bits) for c in range(CYCLES)])
    width = 1 << gate_bits
    height = traj << nbits - gate_bits
    vmem = pl.BlockSpec(memory_space=pltpu.VMEM)
    sizes = (traj, nbits, gate_bits, grp_bits, dev_bits)
    return pl.pallas_call(
        functools.partial(kernel, sizes),
        out_shape=jax.ShapeDtypeStruct(state.shape, state.dtype),
        in_specs=[vmem, vmem, vmem],
        out_specs=vmem,
        scratch_shapes=[
            pltpu.VMEM((2, height, width), jnp.float32),
            pltpu.VMEM((CYCLES, 2, height, width), jnp.float32),
            pltpu.VMEM((CYCLES, 2, height, width), jnp.float32),
            pltpu.SemaphoreType.DMA((CYCLES, 1 << dev_bits)),
            pltpu.SemaphoreType.DMA((CYCLES, 1 << dev_bits)),
        ],
        compiler_params=pltpu.CompilerParams(
            collective_id=0, has_side_effects=True, vmem_limit_bytes=32 << 20
        ),
    )(state, gates, plan)


def solution(mesh):
    placed = (P(None, None, ("grp", "dev")), P(), P())
    return jax.shard_map(
        on_device,
        mesh=mesh,
        in_specs=placed,
        out_specs=P(None, None, ("grp", "dev")),
        check_vma=False,
    )
```

```python
import functools

import jax
import jax.numpy as jnp
from jax import lax
from jax.experimental import pallas as pl
from jax.experimental.pallas import tpu as pltpu
from jax.sharding import PartitionSpec as P

MESH = pl.DeviceIdType.MESH
CYCLES = 2
GATES = 4


def permutation_plan(perm, nbits, gate_bits, lane):
    row_bits = nbits - gate_bits
    shared = gate_bits - row_bits
    leaving = sum(1 << perm[b] for b in range(gate_bits, nbits))
    enters = [1 - (leaving >> (gate_bits + j) & 1) for j in range(row_bits)]
    open_slots = closed_slots = 0
    open_at = closed_at = 0
    for j in range(gate_bits):
        is_open = enters[j] if j < row_bits else 0
        open_slots = open_slots + (j * is_open << open_at)
        closed_slots = closed_slots + (j * (1 - is_open) << closed_at)
        open_at = open_at + 4 * is_open
        closed_at = closed_at + 4 * (1 - is_open)
    slot = []
    position_low = position_high = 0
    for q in range(gate_bits):
        leaves = leaving >> q & 1
        here = jnp.where(leaves == 1, open_slots, closed_slots) & 15
        open_slots = open_slots >> 4 * leaves
        closed_slots = closed_slots >> 4 * (1 - leaves)
        slot.append(here)
        position_low = position_low + (here + gate_bits * leaves << 4 * q)
    for j in range(row_bits):
        position_high = position_high + (gate_bits + j - gate_bits * enters[j] << 4 * j)
    placed = []
    for b in range(nbits):
        low = position_low >> 4 * jnp.minimum(perm[b], gate_bits - 1) & 15
        high = position_high >> 4 * jnp.maximum(perm[b] - gate_bits, 0) & 15
        placed.append(jnp.where(perm[b] < gate_bits, low, high))

    def lane_map(places):
        return sum((lane >> k & 1) << place for k, place in enumerate(places))

    high_place = list(range(row_bits, gate_bits)) + [place - gate_bits for place in placed[gate_bits:]]
    maps = [lane_map(slot), lane_map(placed[:gate_bits]), lane_map(high_place)]
    return maps, [enter == 1 for enter in enters]


def split(x):
    high = x.astype(jnp.bfloat16)
    low = (x - high.astype(jnp.float32)).astype(jnp.bfloat16)
    return high, low


def dot(a, b, contract):
    return lax.dot_general(a, b, (contract, ((), ())), preferred_element_type=jnp.float32)


NT = ((1,), (1,))
NN = ((1,), (0,))


def swap_lane_bit(first, second, bit, lane, condition=None):
    width = first.shape[-1]
    axis = first.ndim - 1
    up = (lane >> bit & 1) == 1
    down = ~up
    if condition is not None:
        up = up & condition
        down = down & condition
    new_first = jnp.where(up, pltpu.roll(second, 1 << bit, axis), first)
    new_second = jnp.where(down, pltpu.roll(first, width - (1 << bit), axis), second)
    return new_first, new_second


def one_hot(lane_map):
    width = lane_map.shape[-1]
    rows = lax.broadcasted_iota(jnp.int32, (width, width), 0)
    return jnp.where(rows == lane_map, 1.0, 0.0).astype(jnp.bfloat16)


def gate_matrix(real, imag, columns):
    width = real.shape[-1]
    re_high, re_low = split(real)
    im_high, im_low = split(imag)
    if columns is not None:
        stack = jnp.concatenate([re_high, re_low, im_high, im_low])
        moved = dot(stack, columns, NT).astype(jnp.bfloat16)
        re_high, re_low, im_high, im_low = [moved[i * width : (i + 1) * width] for i in range(4)]

    def whole(re, im):
        return jnp.concatenate(
            [jnp.concatenate([re, -im], axis=1), jnp.concatenate([im, re], axis=1)], axis=0
        )

    return whole(re_high, im_high), whole(re_low, im_low)


def kernel(
    sizes,
    state_hbm,
    gates_hbm,
    perm_hbm,
    out_ref,
    state_ref,
    gates_ref,
    perm_ref,
    work,
    sent,
    landed,
    send_sem,
    recv_sem,
    load_sem,
):
    traj, nbits, gate_bits, grp_bits, dev_bits = sizes
    width = 1 << gate_bits
    row_bits = nbits - gate_bits
    shared = gate_bits - row_bits
    rows = 1 << row_bits
    blocks = 1 << dev_bits
    top = blocks // 2
    wide = dev_bits > row_bits
    grp = lax.axis_index("grp")
    dev = lax.axis_index("dev")
    grp_low = grp % 2
    grp_next = grp // 2 % 2
    grp_rest = grp // 4 * 4
    dev_top = dev // top
    dev_low = dev % top

    def targets(cycle, step):
        low = (dev_low ^ (step % top)) if step % top else dev_low
        high = 1 - grp_next if step // top else grp_next
        block = high * top + low
        if cycle == 0:
            return block, grp_rest + high * 2 + grp_low, grp_next * top + low, dev
        return block, grp_rest + high * 2 + grp_next, dev_top * top + low, grp_low * top + dev_low

    self_sent = [dev_top == grp_next, grp_low == grp_next]

    barrier = pltpu.get_barrier_semaphore()
    for step in range(blocks):
        low = (dev_low ^ (step % top)) if step % top else dev_low
        high = step // top
        source_high = 1 - dev_top if high else dev_top
        first = (grp_rest + dev_top * 2 + grp_low, source_high * top + low)
        source_low = 1 - grp_low if high else grp_low
        second = (grp_rest + grp_low * 2 + source_low, dev_top * top + low)

        def tell(device):
            pl.semaphore_signal(barrier, inc=1, device_id=device, device_id_type=MESH)

        if step:
            tell(first)
            tell(second)
        else:
            pl.when(dev_top != grp_next)(functools.partial(tell, first))
            pl.when(grp_low != grp_next)(functools.partial(tell, second))

    loads = [
        pltpu.make_async_copy(perm_hbm, perm_ref, load_sem.at[0]),
        pltpu.make_async_copy(state_hbm, state_ref, load_sem.at[1]),
    ]
    for cycle in range(CYCLES):
        for which in range(GATES):
            sem = load_sem.at[2 + GATES * cycle + which]
            loads.append(
                pltpu.make_async_copy(gates_hbm.at[cycle, which], gates_ref.at[cycle, which], sem)
            )
    for load in loads:
        load.start()

    lane = lax.broadcasted_iota(jnp.int32, (1, width), 1)
    fixed = one_hot((lane % (1 << shared)) * rows + lane // (1 << shared))

    def low_matrix(cycle, which, lane_map):
        columns = None if lane_map is None else one_hot(lane_map)
        loads[2 + GATES * cycle + which].wait()
        return gate_matrix(gates_ref[cycle, which, 0], gates_ref[cycle, which, 1], columns)

    def high_matrix(cycle, which, columns):
        parts = []
        loads[2 + GATES * cycle + which].wait()
        for part in range(2):
            parts.append(
                jnp.concatenate(
                    [
                        gates_ref[cycle, which, part, pl.ds(a, rows, stride=1 << shared), :]
                        for a in range(1 << shared)
                    ]
                )
            )
        return gate_matrix(parts[0], parts[1], columns)

    def apply_low(x, matrix):
        high, low = split(jnp.concatenate([x[0], x[1]], axis=1))
        m_high, m_low = matrix
        y = dot(high, m_high, NT) + (dot(low, m_high, NT) + dot(high, m_low, NT))
        return y[:, :width], y[:, width:]

    def swap_traj(planes):
        planes = list(planes)
        for bit in range(shared):
            for t in range(len(planes)):
                if not t >> bit & 1:
                    o = t | 1 << bit
                    planes[t], planes[o] = swap_lane_bit(planes[t], planes[o], row_bits + bit, lane)
        return planes

    def apply_high(source, matrix, write):
        per = 1 << shared
        operand = []
        for part in range(2):
            planes = [source[part, pl.ds(t, rows, stride=traj), :] for t in range(traj)]
            planes = swap_traj(planes)
            operand.append(
                jnp.concatenate(
                    [jnp.concatenate(planes[g : g + per], axis=0) for g in range(0, traj, per)], axis=1
                )
            )
        high, low = split(jnp.concatenate(operand, axis=0))
        m_high, m_low = matrix
        y = dot(m_high, high, NN) + (dot(m_low, high, NN) + dot(m_high, low, NN))
        for part in range(2):
            planes = [
                y[part * width + a * rows : part * width + (a + 1) * rows, g * width : (g + 1) * width]
                for g in range(traj // per)
                for a in range(per)
            ]
            planes = swap_traj(planes)
            for t in range(traj):
                write[part, pl.ds(t, rows, stride=traj), :] = planes[t]

    def local_part(x, plan, cycle, matrices):
        maps, conditions = plan
        lanes = one_hot(maps[0])
        moved = []
        for part in range(2):
            high, low = split(x[part])
            y = dot(high, lanes, NT) + dot(low, lanes, NT)
            tiles = [y[r * traj : (r + 1) * traj] for r in range(rows)]
            for j in range(row_bits):
                for r in range(rows):
                    if not r >> j & 1:
                        o = r | 1 << j
                        tiles[r], tiles[o] = swap_lane_bit(tiles[r], tiles[o], j, lane, conditions[j])
            moved.append(jnp.concatenate(tiles))
        y = apply_low(moved, matrices[0])
        work[0] = y[0]
        work[1] = y[1]
        apply_high(work, matrices[1], work)
        y = apply_low([work[0], work[1]], matrices[2])
        if wide:
            y = swap_lane_bit(y[0], y[1], gate_bits - 1, lane)
        sent[cycle, 0] = y[0]
        sent[cycle, 1] = y[1]

    def plan_of(cycle):
        return permutation_plan([perm_ref[cycle, b] for b in range(nbits)], nbits, gate_bits, lane)

    def matrices_of(cycle, plan):
        maps, _ = plan
        return (
            low_matrix(cycle, 0, maps[1]),
            high_matrix(cycle, 1, one_hot(maps[2])),
            low_matrix(cycle, 2, None),
        )

    def view(ref, cycle, block):
        if wide:
            start = pl.multiple_of(block // 2 * traj, traj)
            return ref.at[cycle, pl.ds(block % 2, 1), pl.ds(start, traj), :]
        depth = rows * traj // blocks
        start = pl.multiple_of(block * depth, depth)
        return ref.at[cycle, :, pl.ds(start, depth), :]

    def remote(cycle, step):
        block, to_grp, to_dev, slot = targets(cycle, step)
        return pltpu.make_async_remote_copy(
            src_ref=view(sent, cycle, block),
            dst_ref=view(landed, cycle, slot),
            send_sem=send_sem.at[cycle, step],
            recv_sem=recv_sem.at[cycle, slot],
            device_id=(to_grp, to_dev),
            device_id_type=MESH,
        )

    def stay(cycle):
        block, _, _, slot = targets(cycle, 0)
        return pltpu.make_async_copy(
            view(sent, cycle, block), view(landed, cycle, slot), recv_sem.at[cycle, slot]
        )

    def start(cycle):
        for step in range(blocks - 1, 0, -1):
            remote(cycle, step).start()

        @pl.when(self_sent[cycle])
        def _():
            stay(cycle).start()

        @pl.when(jnp.logical_not(self_sent[cycle]))
        def _():
            remote(cycle, 0).start()

    def finish(cycle):
        for slot in range(blocks):
            pltpu.make_async_copy(
                view(landed, cycle, slot), view(landed, cycle, slot), recv_sem.at[cycle, slot]
            ).wait()

    def finish_sends(cycle):
        for step in range(1, blocks):
            remote(cycle, step).wait_send()

        @pl.when(jnp.logical_not(self_sent[cycle]))
        def _():
            remote(cycle, 0).wait_send()

    def unwiden(cycle):
        if wide:
            y = swap_lane_bit(landed[cycle, 0], landed[cycle, 1], gate_bits - 1, lane)
            landed[cycle, 0] = y[0]
            landed[cycle, 1] = y[1]

    loads[0].wait()
    plan = plan_of(0)
    loads[1].wait()
    x = [
        jnp.concatenate([state_ref[part, :, r * width : (r + 1) * width] for r in range(rows)])
        for part in range(2)
    ]
    local_part(x, plan, 0, matrices_of(0, plan))
    others = 2 * (blocks - 1) + jnp.where(self_sent[0], 0, 1) + jnp.where(self_sent[1], 0, 1)
    pl.semaphore_wait(barrier, others)
    start(0)
    last = high_matrix(0, 3, fixed)
    plan = plan_of(1)
    following = matrices_of(1, plan)
    finish(0)
    unwiden(0)
    apply_high(landed.at[0], last, work)
    local_part([work[0], work[1]], plan, 1, following)
    start(1)
    last = high_matrix(1, 3, fixed)
    finish(1)
    unwiden(1)
    apply_high(landed.at[1], last, work)
    for part in range(2):
        for r in range(rows):
            out_ref[part, :, r * width : (r + 1) * width] = work[part, r * traj : (r + 1) * traj, :]
    finish_sends(0)
    finish_sends(1)


def on_device(state, gates, local_perm):
    traj = state.shape[1]
    nbits = state.shape[2].bit_length() - 1
    gate_bits = gates.shape[-1].bit_length() - 1
    grp_bits = lax.axis_size("grp").bit_length() - 1
    dev_bits = lax.axis_size("dev").bit_length() - 1
    width = 1 << gate_bits
    height = traj << nbits - gate_bits
    vmem = pl.BlockSpec(memory_space=pltpu.VMEM)
    sizes = (traj, nbits, gate_bits, grp_bits, dev_bits)
    return pl.pallas_call(
        functools.partial(kernel, sizes),
        out_shape=jax.ShapeDtypeStruct(state.shape, state.dtype),
        in_specs=[pl.BlockSpec(memory_space=pl.ANY)] * 3,
        out_specs=vmem,
        scratch_shapes=[
            pltpu.VMEM(state.shape, state.dtype),
            pltpu.VMEM(gates.shape, gates.dtype),
            pltpu.SMEM(local_perm.shape, local_perm.dtype),
            pltpu.VMEM((2, height, width), jnp.float32),
            pltpu.VMEM((CYCLES, 2, height, width), jnp.float32),
            pltpu.VMEM((CYCLES, 2, height, width), jnp.float32),
            pltpu.SemaphoreType.DMA((CYCLES, 1 << dev_bits)),
            pltpu.SemaphoreType.DMA((CYCLES, 1 << dev_bits)),
            pltpu.SemaphoreType.DMA((2 + GATES * CYCLES,)),
        ],
        compiler_params=pltpu.CompilerParams(
            collective_id=0, has_side_effects=True, vmem_limit_bytes=32 << 20
        ),
    )(state, gates, local_perm)


def solution(mesh):
    placed = (P(None, None, ("grp", "dev")), P(), P())
    return jax.shard_map(
        on_device,
        mesh=mesh,
        in_specs=placed,
        out_specs=P(None, None, ("grp", "dev")),
        check_vma=False,
    )
```

```python
import functools

import jax
import jax.numpy as jnp
from jax import lax
from jax.experimental import pallas as pl
from jax.experimental.pallas import tpu as pltpu
from jax.sharding import PartitionSpec as P

MESH = pl.DeviceIdType.MESH
CYCLES = 2
GATES = 4


def permutation_plan(perm, nbits, gate_bits, lane):
    row_bits = nbits - gate_bits
    shared = gate_bits - row_bits
    leaving = sum(1 << perm[b] for b in range(gate_bits, nbits))
    enters = [1 - (leaving >> (gate_bits + j) & 1) for j in range(row_bits)]
    open_slots = closed_slots = 0
    open_at = closed_at = 0
    for j in range(gate_bits):
        is_open = enters[j] if j < row_bits else 0
        open_slots = open_slots + (j * is_open << open_at)
        closed_slots = closed_slots + (j * (1 - is_open) << closed_at)
        open_at = open_at + 4 * is_open
        closed_at = closed_at + 4 * (1 - is_open)
    slot = []
    position_low = position_high = 0
    for q in range(gate_bits):
        leaves = leaving >> q & 1
        here = jnp.where(leaves == 1, open_slots, closed_slots) & 15
        open_slots = open_slots >> 4 * leaves
        closed_slots = closed_slots >> 4 * (1 - leaves)
        slot.append(here)
        position_low = position_low + (here + gate_bits * leaves << 4 * q)
    for j in range(row_bits):
        position_high = position_high + (gate_bits + j - gate_bits * enters[j] << 4 * j)
    placed = []
    for b in range(nbits):
        low = position_low >> 4 * jnp.minimum(perm[b], gate_bits - 1) & 15
        high = position_high >> 4 * jnp.maximum(perm[b] - gate_bits, 0) & 15
        placed.append(jnp.where(perm[b] < gate_bits, low, high))

    def lane_map(places):
        return sum((lane >> k & 1) << place for k, place in enumerate(places))

    high_place = list(range(row_bits, gate_bits)) + [place - gate_bits for place in placed[gate_bits:]]
    maps = [lane_map(slot), lane_map(placed[:gate_bits]), lane_map(high_place)]
    return maps, [enter == 1 for enter in enters]


def split(x):
    high = x.astype(jnp.bfloat16)
    low = (x - high.astype(jnp.float32)).astype(jnp.bfloat16)
    return high, low


def dot(a, b, contract):
    return lax.dot_general(a, b, (contract, ((), ())), preferred_element_type=jnp.float32)


NT = ((1,), (1,))
NN = ((1,), (0,))


def swap_lane_bit(first, second, bit, lane, condition=None):
    width = first.shape[-1]
    axis = first.ndim - 1
    up = (lane >> bit & 1) == 1
    down = ~up
    if condition is not None:
        up = up & condition
        down = down & condition
    new_first = jnp.where(up, pltpu.roll(second, 1 << bit, axis), first)
    new_second = jnp.where(down, pltpu.roll(first, width - (1 << bit), axis), second)
    return new_first, new_second


def one_hot(lane_map):
    width = lane_map.shape[-1]
    rows = lax.broadcasted_iota(jnp.int32, (width, width), 0)
    return jnp.where(rows == lane_map, 1.0, 0.0).astype(jnp.bfloat16)


def stack_parts(real, imag):
    return jnp.concatenate([*split(real), *split(imag)])


def left_matrix(real, imag, columns):
    width = real.shape[-1]
    moved = dot(stack_parts(real, imag), columns, NT).astype(jnp.bfloat16)
    re_high, re_low, im_high, im_low = [moved[i * width : (i + 1) * width] for i in range(4)]

    def whole(re, im):
        return jnp.concatenate(
            [jnp.concatenate([re, -im], axis=1), jnp.concatenate([im, re], axis=1)], axis=0
        )

    return whole(re_high, im_high), whole(re_low, im_low)


def right_matrix(real, imag, columns):
    width = real.shape[-1]
    moved = dot(columns, stack_parts(real, imag), NT).astype(jnp.bfloat16)
    re_high, re_low, im_high, im_low = [moved[:, i * width : (i + 1) * width] for i in range(4)]

    def whole(re, im):
        return jnp.concatenate(
            [jnp.concatenate([re, im], axis=1), jnp.concatenate([-im, re], axis=1)], axis=0
        )

    return whole(re_high, im_high), whole(re_low, im_low)


def kernel(
    sizes,
    state_hbm,
    gates_hbm,
    perm_hbm,
    out_ref,
    state_ref,
    gates_ref,
    perm_ref,
    work,
    final,
    sent,
    landed,
    send_sem,
    recv_sem,
    load_sem,
):
    traj, nbits, gate_bits, dev_bits, halves = sizes
    width = 1 << gate_bits
    row_bits = nbits - gate_bits
    shared = gate_bits - row_bits
    per = 1 << shared
    rows = 1 << row_bits
    blocks = 1 << dev_bits
    top = blocks // 2
    wide = dev_bits > row_bits
    own_traj = traj // halves
    grp = lax.axis_index("grp")
    dev = lax.axis_index("dev")
    grp_low = grp % 2
    grp_next = grp // 2 % 2
    grp_rest = grp // 4 * 4
    dev_top = dev // top
    dev_low = dev % top

    def targets(cycle, step):
        low = (dev_low ^ (step % top)) if step % top else dev_low
        high = 1 - grp_next if step // top else grp_next
        block = high * top + low
        if cycle == 0:
            return block, grp_rest + high * 2 + grp_low, grp_next * top + low, dev
        return block, grp_rest + high * 2 + grp_next, dev_top * top + low, grp_low * top + dev_low

    self_sent = [dev_top == grp_next, grp_low == grp_next]

    barrier = pltpu.get_barrier_semaphore()
    for step in range(blocks):
        low = (dev_low ^ (step % top)) if step % top else dev_low
        high = step // top
        source_high = 1 - dev_top if high else dev_top
        first = (grp_rest + dev_top * 2 + grp_low, source_high * top + low)
        source_low = 1 - grp_low if high else grp_low
        second = (grp_rest + grp_low * 2 + source_low, dev_top * top + low)

        def tell(device):
            pl.semaphore_signal(barrier, inc=1, device_id=device, device_id_type=MESH)

        if step:
            tell(first)
            tell(second)
        else:
            pl.when(dev_top != grp_next)(functools.partial(tell, first))
            pl.when(grp_low != grp_next)(functools.partial(tell, second))

    loads = [
        pltpu.make_async_copy(perm_hbm, perm_ref, load_sem.at[0]),
        pltpu.make_async_copy(state_hbm, state_ref, load_sem.at[1]),
    ]
    for cycle in range(CYCLES):
        for which in range(GATES):
            sem = load_sem.at[2 + GATES * cycle + which]
            loads.append(
                pltpu.make_async_copy(gates_hbm.at[cycle, which], gates_ref.at[cycle, which], sem)
            )
    for load in loads:
        load.start()

    lane = lax.broadcasted_iota(jnp.int32, (1, width), 1)

    def low_matrix(cycle, which, lane_map):
        loads[2 + GATES * cycle + which].wait()
        return right_matrix(gates_ref[cycle, which, 0], gates_ref[cycle, which, 1], one_hot(lane_map))

    def high_matrix(cycle, which, lane_map):
        loads[2 + GATES * cycle + which].wait()
        parts = [
            jnp.concatenate(
                [gates_ref[cycle, which, part, pl.ds(a, rows, stride=per), :] for a in range(per)]
            )
            for part in range(2)
        ]
        return left_matrix(parts[0], parts[1], one_hot(lane_map))

    def plan_of(cycle):
        return permutation_plan([perm_ref[cycle, b] for b in range(nbits)], nbits, gate_bits, lane)

    def matrices_of(cycle, plan):
        maps, _ = plan
        return (
            low_matrix(cycle, 0, maps[1]),
            high_matrix(cycle, 1, maps[2]),
            low_matrix(cycle, 2, lane),
        )

    def last_matrix(cycle):
        return high_matrix(cycle, 3, (lane % per) * rows + lane // per)


    def apply_low(planes, matrix):
        high, low = split(jnp.concatenate([jnp.concatenate(part) for part in planes], axis=1))
        m_high, m_low = matrix
        y = dot(high, m_high, NN) + (dot(low, m_high, NN) + dot(high, m_low, NN))
        return [
            [y[t * rows : (t + 1) * rows, part * width : (part + 1) * width] for t in range(own_traj)]
            for part in range(2)
        ]

    def swap_traj(planes):
        planes = list(planes)
        for bit in range(shared):
            for t in range(len(planes)):
                if not t >> bit & 1:
                    o = t | 1 << bit
                    planes[t], planes[o] = swap_lane_bit(planes[t], planes[o], row_bits + bit, lane)
        return planes

    def apply_high(planes, matrix):
        operand = []
        for part in planes:
            part = swap_traj(part)
            operand.append(
                jnp.concatenate(
                    [jnp.concatenate(part[g : g + per]) for g in range(0, own_traj, per)], axis=1
                )
            )
        high, low = split(jnp.concatenate(operand))
        m_high, m_low = matrix
        y = dot(m_high, high, NN) + (dot(m_low, high, NN) + dot(m_high, low, NN))
        return [
            swap_traj(
                [
                    y[part * width + a * rows : part * width + (a + 1) * rows, g * width : (g + 1) * width]
                    for g in range(own_traj // per)
                    for a in range(per)
                ]
            )
            for part in range(2)
        ]

    def local_part(x, half, cycle, plan, matrices):
        maps, conditions = plan
        lanes = one_hot(maps[0])
        x = jnp.concatenate(split(x), axis=1)
        y = dot(x, jnp.concatenate([lanes, lanes], axis=1), NT)
        height = 2 * own_traj
        tiles = [y[r * height : (r + 1) * height] for r in range(rows)]
        for j in range(row_bits):
            for r in range(rows):
                if not r >> j & 1:
                    o = r | 1 << j
                    tiles[r], tiles[o] = swap_lane_bit(tiles[r], tiles[o], j, lane, conditions[j])
        for r in range(rows):
            work[half, r * height : (r + 1) * height, :] = tiles[r]
        planes = [
            [work[half, pl.ds(part * own_traj + t, rows, stride=height), :] for t in range(own_traj)]
            for part in range(2)
        ]
        planes = apply_low(planes, matrices[0])
        planes = apply_high(planes, matrices[1])
        planes = apply_low(planes, matrices[2])
        if wide:
            pairs = [swap_lane_bit(a, b, gate_bits - 1, lane) for a, b in zip(*planes)]
            planes = list(zip(*pairs))
        for part in range(2):
            for t in range(own_traj):
                sent[cycle, half, part, pl.ds(t, rows, stride=own_traj), :] = planes[part][t]

    def last_part(half, cycle, matrix):
        planes = [
            [landed[cycle, half, part, pl.ds(t, rows, stride=own_traj), :] for t in range(own_traj)]
            for part in range(2)
        ]
        if wide:
            pairs = [swap_lane_bit(a, b, gate_bits - 1, lane) for a, b in zip(*planes)]
            planes = list(zip(*pairs))
        return apply_high(planes, matrix)

    def view(ref, cycle, half, block):
        if wide:
            start = pl.multiple_of(block // 2 * own_traj, own_traj)
            return ref.at[cycle, half, pl.ds(block % 2, 1), pl.ds(start, own_traj), :]
        depth = rows * own_traj // blocks
        start = pl.multiple_of(block * depth, depth)
        return ref.at[cycle, half, :, pl.ds(start, depth), :]

    def remote(cycle, half, step):
        block, to_grp, to_dev, slot = targets(cycle, step)
        return pltpu.make_async_remote_copy(
            src_ref=view(sent, cycle, half, block),
            dst_ref=view(landed, cycle, half, slot),
            send_sem=send_sem.at[cycle, half, step],
            recv_sem=recv_sem.at[cycle, half],
            device_id=(to_grp, to_dev),
            device_id_type=MESH,
        )

    def start(cycle, half):
        for step in range(blocks - 1, 0, -1):
            remote(cycle, half, step).start()

        @pl.when(self_sent[cycle])
        def _():
            block, _, _, slot = targets(cycle, 0)
            pltpu.make_async_copy(
                view(sent, cycle, half, block), view(landed, cycle, half, slot), recv_sem.at[cycle, half]
            ).start()

        @pl.when(jnp.logical_not(self_sent[cycle]))
        def _():
            remote(cycle, half, 0).start()

    def finish(cycle, half):
        whole = landed.at[cycle, half]
        pltpu.make_async_copy(whole, whole, recv_sem.at[cycle, half]).wait()

    def finish_sends(cycle, half):
        for step in range(1, blocks):
            remote(cycle, half, step).wait_send()

        @pl.when(jnp.logical_not(self_sent[cycle]))
        def _():
            remote(cycle, half, 0).wait_send()

    loads[0].wait()
    plan = plan_of(0)
    loads[1].wait()
    matrices = matrices_of(0, plan)
    for half in range(halves):
        tiles = []
        for r in range(rows):
            for part in range(2):
                tiles.append(
                    state_ref[
                        part, half * own_traj : (half + 1) * own_traj, r * width : (r + 1) * width
                    ]
                )
        local_part(jnp.concatenate(tiles), half, 0, plan, matrices)
        if half == 0:
            others = 2 * (blocks - 1) + jnp.where(self_sent[0], 0, 1) + jnp.where(self_sent[1], 0, 1)
            pl.semaphore_wait(barrier, others)
        start(0, half)
    last = last_matrix(0)
    plan = plan_of(1)
    matrices = matrices_of(1, plan)
    for half in range(halves):
        finish(0, half)
        planes = last_part(half, 0, last)
        height = 2 * own_traj
        for part in range(2):
            for t in range(own_traj):
                work[half, pl.ds(part * own_traj + t, rows, stride=height), :] = planes[part][t]
        local_part(work[half], half, 1, plan, matrices)
        start(1, half)
    last = last_matrix(1)
    for half in range(halves):
        finish(1, half)
        planes = last_part(half, 1, last)
        for part in range(2):
            for t in range(own_traj):
                final[part, pl.ds(half * own_traj + t, rows, stride=traj), :] = planes[part][t]
    for part in range(2):
        for r in range(rows):
            out_ref[part, :, r * width : (r + 1) * width] = final[part, r * traj : (r + 1) * traj, :]
    for cycle in range(CYCLES):
        for half in range(halves):
            finish_sends(cycle, half)


def on_device(state, gates, local_perm):
    traj = state.shape[1]
    nbits = state.shape[2].bit_length() - 1
    gate_bits = gates.shape[-1].bit_length() - 1
    dev_bits = lax.axis_size("dev").bit_length() - 1
    width = 1 << gate_bits
    rows = 1 << nbits - gate_bits
    halves = 2 if (rows * traj // 2 >> dev_bits) % 8 == 0 else 1
    sizes = (traj, nbits, gate_bits, dev_bits, halves)
    buffer = pltpu.VMEM((CYCLES, halves, 2, rows * traj // halves, width), jnp.float32)
    return pl.pallas_call(
        functools.partial(kernel, sizes),
        out_shape=jax.ShapeDtypeStruct(state.shape, state.dtype),
        in_specs=[pl.BlockSpec(memory_space=pltpu.HBM)] * 3,
        out_specs=pl.BlockSpec(memory_space=pltpu.VMEM),
        scratch_shapes=[
            pltpu.VMEM(state.shape, state.dtype),
            pltpu.VMEM(gates.shape, gates.dtype),
            pltpu.SMEM(local_perm.shape, local_perm.dtype),
            pltpu.VMEM((halves, 2 * rows * traj // halves, width), jnp.float32),
            pltpu.VMEM((2, rows * traj, width), jnp.float32),
            buffer,
            buffer,
            pltpu.SemaphoreType.DMA((CYCLES, halves, 1 << dev_bits)),
            pltpu.SemaphoreType.DMA((CYCLES, halves)),
            pltpu.SemaphoreType.DMA((2 + GATES * CYCLES,)),
        ],
        compiler_params=pltpu.CompilerParams(
            collective_id=0, has_side_effects=True, vmem_limit_bytes=60 << 20
        ),
    )(state, gates, local_perm)


def solution(mesh):
    placed = (P(None, None, ("grp", "dev")), P(), P())
    return jax.shard_map(
        on_device,
        mesh=mesh,
        in_specs=placed,
        out_specs=P(None, None, ("grp", "dev")),
        check_vma=False,
    )
```

```python
import functools

import jax
import jax.numpy as jnp
from jax import lax
from jax.experimental import pallas as pl
from jax.experimental.pallas import tpu as pltpu
from jax.sharding import PartitionSpec as P

MESH = pl.DeviceIdType.MESH
CYCLES = 2
GATES = 4


def permutation_plan(perm, nbits, gate_bits, lane):
    row_bits = nbits - gate_bits
    shared = gate_bits - row_bits
    leaving = sum(1 << perm[b] for b in range(gate_bits, nbits))
    enters = [1 - (leaving >> (gate_bits + j) & 1) for j in range(row_bits)]
    open_slots = closed_slots = 0
    open_at = closed_at = 0
    for j in range(gate_bits):
        is_open = enters[j] if j < row_bits else 0
        open_slots = open_slots + (j * is_open << open_at)
        closed_slots = closed_slots + (j * (1 - is_open) << closed_at)
        open_at = open_at + 4 * is_open
        closed_at = closed_at + 4 * (1 - is_open)
    slot = []
    position_low = position_high = 0
    for q in range(gate_bits):
        leaves = leaving >> q & 1
        here = jnp.where(leaves == 1, open_slots, closed_slots) & 15
        open_slots = open_slots >> 4 * leaves
        closed_slots = closed_slots >> 4 * (1 - leaves)
        slot.append(here)
        position_low = position_low + (here + gate_bits * leaves << 4 * q)
    for j in range(row_bits):
        position_high = position_high + (gate_bits + j - gate_bits * enters[j] << 4 * j)
    placed = []
    for b in range(nbits):
        low = position_low >> 4 * jnp.minimum(perm[b], gate_bits - 1) & 15
        high = position_high >> 4 * jnp.maximum(perm[b] - gate_bits, 0) & 15
        placed.append(jnp.where(perm[b] < gate_bits, low, high))

    def lane_map(places):
        return sum((lane >> k & 1) << place for k, place in enumerate(places))

    high_place = list(range(row_bits, gate_bits)) + [place - gate_bits for place in placed[gate_bits:]]
    maps = [lane_map(slot), lane_map(placed[:gate_bits]), lane_map(high_place)]
    return maps, [enter == 1 for enter in enters]


def split(x):
    high = x.astype(jnp.bfloat16)
    low = (x - high.astype(jnp.float32)).astype(jnp.bfloat16)
    return high, low


def dot(a, b, contract):
    return lax.dot_general(a, b, (contract, ((), ())), preferred_element_type=jnp.float32)


NT = ((1,), (1,))
NN = ((1,), (0,))


def swap_lane_bit(first, second, bit, lane, condition=None):
    width = first.shape[-1]
    axis = first.ndim - 1
    up = (lane >> bit & 1) == 1
    down = ~up
    if condition is not None:
        up = up & condition
        down = down & condition
    new_first = jnp.where(up, pltpu.roll(second, 1 << bit, axis), first)
    new_second = jnp.where(down, pltpu.roll(first, width - (1 << bit), axis), second)
    return new_first, new_second


def one_hot(lane_map):
    width = lane_map.shape[-1]
    rows = lax.broadcasted_iota(jnp.int32, (width, width), 0)
    return jnp.where(rows == lane_map, 1.0, 0.0).astype(jnp.bfloat16)


def stack_parts(real, imag):
    return jnp.concatenate([*split(real), *split(imag)])


def left_matrix(real, imag, columns):
    width = real.shape[-1]
    moved = dot(stack_parts(real, imag), columns, NT).astype(jnp.bfloat16)
    re_high, re_low, im_high, im_low = [moved[i * width : (i + 1) * width] for i in range(4)]

    def whole(re, im):
        return jnp.concatenate(
            [jnp.concatenate([re, -im], axis=1), jnp.concatenate([im, re], axis=1)], axis=0
        )

    return whole(re_high, im_high), whole(re_low, im_low)


def right_matrix(real, imag, columns):
    width = real.shape[-1]
    moved = dot(columns, stack_parts(real, imag), NT).astype(jnp.bfloat16)
    re_high, re_low, im_high, im_low = [moved[:, i * width : (i + 1) * width] for i in range(4)]

    def whole(re, im):
        return jnp.concatenate(
            [jnp.concatenate([re, im], axis=1), jnp.concatenate([-im, re], axis=1)], axis=0
        )

    return whole(re_high, im_high), whole(re_low, im_low)


def kernel(
    sizes,
    state_hbm,
    gates_hbm,
    perm_hbm,
    out_ref,
    state_ref,
    gates_ref,
    perm_ref,
    work,
    final,
    sent,
    landed,
    send_sem,
    recv_sem,
    load_sem,
):
    traj, nbits, gate_bits, dev_bits, halves = sizes
    width = 1 << gate_bits
    row_bits = nbits - gate_bits
    shared = gate_bits - row_bits
    per = 1 << shared
    rows = 1 << row_bits
    blocks = 1 << dev_bits
    top = blocks // 2
    wide = dev_bits > row_bits
    own_traj = traj // halves
    grp = lax.axis_index("grp")
    dev = lax.axis_index("dev")
    grp_low = grp % 2
    grp_next = grp // 2 % 2
    grp_rest = grp // 4 * 4
    dev_top = dev // top
    dev_low = dev % top


    def targets(cycle, step):
        low = (dev_low ^ (step % top)) if step % top else dev_low
        own = grp_next if cycle else grp_low
        high = 1 - own if step // top else own
        block = high * top + low
        if cycle == 0:
            return block, grp_rest + grp_low * 2 + high, grp_next * top + low, dev
        return block, grp_rest + high * 2 + grp_low, dev_top * top + low, grp_next * top + dev_low

    stays = jnp.logical_and(grp_low == grp_next, grp_next == dev_top)

    barrier = pltpu.get_barrier_semaphore()
    for step in range(blocks):
        low = (dev_low ^ (step % top)) if step % top else dev_low
        high = step // top
        source_top = 1 - dev_top if high else dev_top
        first = (grp_rest + dev_top * 2 + grp_next, source_top * top + low)
        source_next = 1 - grp_next if high else grp_next
        second = (grp_rest + source_next * 2 + grp_low, dev_top * top + low)

        def tell(device):
            pl.semaphore_signal(barrier, inc=1, device_id=device, device_id_type=MESH)

        if step:
            tell(first)
            tell(second)
        else:
            pl.when(jnp.logical_not(stays))(functools.partial(tell, first))

    loads = [
        pltpu.make_async_copy(perm_hbm, perm_ref, load_sem.at[0]),
        pltpu.make_async_copy(state_hbm, state_ref, load_sem.at[1]),
    ]
    for cycle in range(CYCLES):
        for which in range(GATES):
            sem = load_sem.at[2 + GATES * cycle + which]
            loads.append(
                pltpu.make_async_copy(gates_hbm.at[cycle, which], gates_ref.at[cycle, which], sem)
            )
    for load in loads:
        load.start()

    lane = lax.broadcasted_iota(jnp.int32, (1, width), 1)

    def low_matrix(cycle, which, lane_map):
        loads[2 + GATES * cycle + which].wait()
        return right_matrix(gates_ref[cycle, which, 0], gates_ref[cycle, which, 1], one_hot(lane_map))

    def high_matrix(cycle, which, lane_map):
        loads[2 + GATES * cycle + which].wait()
        parts = [
            jnp.concatenate(
                [gates_ref[cycle, which, part, pl.ds(a, rows, stride=per), :] for a in range(per)]
            )
            for part in range(2)
        ]
        return left_matrix(parts[0], parts[1], one_hot(lane_map))

    def plan_of(cycle):
        return permutation_plan([perm_ref[cycle, b] for b in range(nbits)], nbits, gate_bits, lane)

    def matrices_of(cycle, plan):
        maps, _ = plan
        return (
            low_matrix(cycle, 0, maps[1]),
            high_matrix(cycle, 1, maps[2]),
            low_matrix(cycle, 2, lane),
        )

    def last_matrix(cycle):
        return high_matrix(cycle, 3, (lane % per) * rows + lane // per)


    def apply_low(planes, matrix):
        high, low = split(jnp.concatenate([jnp.concatenate(part) for part in planes], axis=1))
        m_high, m_low = matrix
        y = dot(high, m_high, NN) + (dot(low, m_high, NN) + dot(high, m_low, NN))
        return [
            [y[t * rows : (t + 1) * rows, part * width : (part + 1) * width] for t in range(own_traj)]
            for part in range(2)
        ]

    def swap_traj(planes):
        planes = list(planes)
        for bit in range(shared):
            for t in range(len(planes)):
                if not t >> bit & 1:
                    o = t | 1 << bit
                    planes[t], planes[o] = swap_lane_bit(planes[t], planes[o], row_bits + bit, lane)
        return planes

    def apply_high(planes, matrix):
        operand = []
        for part in planes:
            part = swap_traj(part)
            operand.append(
                jnp.concatenate(
                    [jnp.concatenate(part[g : g + per]) for g in range(0, own_traj, per)], axis=1
                )
            )
        high, low = split(jnp.concatenate(operand))
        m_high, m_low = matrix
        y = dot(m_high, high, NN) + (dot(m_low, high, NN) + dot(m_high, low, NN))
        return [
            swap_traj(
                [
                    y[part * width + a * rows : part * width + (a + 1) * rows, g * width : (g + 1) * width]
                    for g in range(own_traj // per)
                    for a in range(per)
                ]
            )
            for part in range(2)
        ]

    def local_part(x, half, cycle, plan, matrices):
        maps, conditions = plan
        lanes = one_hot(maps[0])
        x = jnp.concatenate(split(x), axis=1)
        y = dot(x, jnp.concatenate([lanes, lanes], axis=1), NT)
        height = 2 * own_traj
        tiles = [y[r * height : (r + 1) * height] for r in range(rows)]
        for j in range(row_bits):
            for r in range(rows):
                if not r >> j & 1:
                    o = r | 1 << j
                    tiles[r], tiles[o] = swap_lane_bit(tiles[r], tiles[o], j, lane, conditions[j])
        for r in range(rows):
            work[half, r * height : (r + 1) * height, :] = tiles[r]
        planes = [
            [work[half, pl.ds(part * own_traj + t, rows, stride=height), :] for t in range(own_traj)]
            for part in range(2)
        ]
        planes = apply_low(planes, matrices[0])
        planes = apply_high(planes, matrices[1])
        planes = apply_low(planes, matrices[2])
        if wide:
            pairs = [swap_lane_bit(a, b, gate_bits - 1, lane) for a, b in zip(*planes)]
            planes = list(zip(*pairs))
        for part in range(2):
            for t in range(own_traj):
                sent[cycle, half, part, pl.ds(t, rows, stride=own_traj), :] = planes[part][t]

    def last_part(half, cycle, matrix):
        planes = [
            [landed[cycle, half, part, pl.ds(t, rows, stride=own_traj), :] for t in range(own_traj)]
            for part in range(2)
        ]
        if wide:
            pairs = [swap_lane_bit(a, b, gate_bits - 1, lane) for a, b in zip(*planes)]
            planes = list(zip(*pairs))
        return apply_high(planes, matrix)

    def view(ref, cycle, half, block):
        if wide:
            start = pl.multiple_of(block // 2 * own_traj, own_traj)
            return ref.at[cycle, half, pl.ds(block % 2, 1), pl.ds(start, own_traj), :]
        depth = rows * own_traj // blocks
        start = pl.multiple_of(block * depth, depth)
        return ref.at[cycle, half, :, pl.ds(start, depth), :]

    def remote(cycle, half, step):
        block, to_grp, to_dev, slot = targets(cycle, step)
        return pltpu.make_async_remote_copy(
            src_ref=view(sent, cycle, half, block),
            dst_ref=view(landed, cycle, half, slot),
            send_sem=send_sem.at[cycle, half, step],
            recv_sem=recv_sem.at[cycle, half],
            device_id=(to_grp, to_dev),
            device_id_type=MESH,
        )

    def start(cycle, half):
        for step in range(blocks - 1, 0, -1):
            remote(cycle, half, step).start()

        def keep():
            block, _, _, slot = targets(cycle, 0)
            pltpu.make_async_copy(
                view(sent, cycle, half, block), view(landed, cycle, half, slot), recv_sem.at[cycle, half]
            ).start()

        if cycle:
            keep()
        else:
            pl.when(stays)(keep)
            pl.when(jnp.logical_not(stays))(remote(cycle, half, 0).start)

    def finish(cycle, half):
        whole = landed.at[cycle, half]
        pltpu.make_async_copy(whole, whole, recv_sem.at[cycle, half]).wait()

    def finish_sends(cycle, half):
        for step in range(1, blocks):
            remote(cycle, half, step).wait_send()

        if not cycle:
            pl.when(jnp.logical_not(stays))(remote(cycle, half, 0).wait_send)

    loads[0].wait()
    plan = plan_of(0)
    loads[1].wait()
    matrices = matrices_of(0, plan)
    for half in range(halves):
        tiles = []
        for r in range(rows):
            for part in range(2):
                tiles.append(
                    state_ref[
                        part, half * own_traj : (half + 1) * own_traj, r * width : (r + 1) * width
                    ]
                )
        local_part(jnp.concatenate(tiles), half, 0, plan, matrices)
        if half == 0:
            pl.semaphore_wait(barrier, 2 * (blocks - 1) + jnp.where(stays, 0, 1))
        start(0, half)
    last = last_matrix(0)
    plan = plan_of(1)
    matrices = matrices_of(1, plan)
    for half in range(halves):
        finish(0, half)
        planes = last_part(half, 0, last)
        height = 2 * own_traj
        for part in range(2):
            for t in range(own_traj):
                work[half, pl.ds(part * own_traj + t, rows, stride=height), :] = planes[part][t]
        local_part(work[half], half, 1, plan, matrices)
        start(1, half)
    last = last_matrix(1)
    for half in range(halves):
        finish(1, half)
        planes = last_part(half, 1, last)
        for part in range(2):
            for t in range(own_traj):
                final[part, pl.ds(half * own_traj + t, rows, stride=traj), :] = planes[part][t]
    for part in range(2):
        for r in range(rows):
            out_ref[part, :, r * width : (r + 1) * width] = final[part, r * traj : (r + 1) * traj, :]
    for cycle in range(CYCLES):
        for half in range(halves):
            finish_sends(cycle, half)


def on_device(state, gates, local_perm):
    traj = state.shape[1]
    nbits = state.shape[2].bit_length() - 1
    gate_bits = gates.shape[-1].bit_length() - 1
    dev_bits = lax.axis_size("dev").bit_length() - 1
    width = 1 << gate_bits
    rows = 1 << nbits - gate_bits
    halves = 2 if (rows * traj // 2 >> dev_bits) % 8 == 0 else 1
    sizes = (traj, nbits, gate_bits, dev_bits, halves)
    buffer = pltpu.VMEM((CYCLES, halves, 2, rows * traj // halves, width), jnp.float32)
    return pl.pallas_call(
        functools.partial(kernel, sizes),
        out_shape=jax.ShapeDtypeStruct(state.shape, state.dtype),
        in_specs=[pl.BlockSpec(memory_space=pltpu.HBM)] * 3,
        out_specs=pl.BlockSpec(memory_space=pltpu.VMEM),
        scratch_shapes=[
            pltpu.VMEM(state.shape, state.dtype),
            pltpu.VMEM(gates.shape, gates.dtype),
            pltpu.SMEM(local_perm.shape, local_perm.dtype),
            pltpu.VMEM((halves, 2 * rows * traj // halves, width), jnp.float32),
            pltpu.VMEM((2, rows * traj, width), jnp.float32),
            buffer,
            buffer,
            pltpu.SemaphoreType.DMA((CYCLES, halves, 1 << dev_bits)),
            pltpu.SemaphoreType.DMA((CYCLES, halves)),
            pltpu.SemaphoreType.DMA((2 + GATES * CYCLES,)),
        ],
        compiler_params=pltpu.CompilerParams(
            collective_id=0, has_side_effects=True, vmem_limit_bytes=32 << 20
        ),
    )(*[pltpu.with_memory_space_constraint(x, pltpu.HBM) for x in (state, gates, local_perm)])


def solution(mesh):
    placed = (P(None, None, ("grp", "dev")), P(), P())
    return jax.shard_map(
        on_device,
        mesh=mesh,
        in_specs=placed,
        out_specs=P(None, None, ("grp", "dev")),
        check_vma=False,
    )
```

```python
import functools

import jax
import jax.numpy as jnp
from jax import lax
from jax.experimental import pallas as pl
from jax.experimental.pallas import tpu as pltpu
from jax.sharding import PartitionSpec as P

MESH = pl.DeviceIdType.MESH
CYCLES = 2
GATES = 4


def permutation_plan(perm, nbits, gate_bits, lane):
    row_bits = nbits - gate_bits
    shared = gate_bits - row_bits
    leaving = sum(1 << perm[b] for b in range(gate_bits, nbits))
    enters = [1 - (leaving >> (gate_bits + j) & 1) for j in range(row_bits)]
    open_slots = closed_slots = 0
    open_at = closed_at = 0
    for j in range(gate_bits):
        is_open = enters[j] if j < row_bits else 0
        open_slots = open_slots + (j * is_open << open_at)
        closed_slots = closed_slots + (j * (1 - is_open) << closed_at)
        open_at = open_at + 4 * is_open
        closed_at = closed_at + 4 * (1 - is_open)
    slot = []
    position_low = position_high = 0
    for q in range(gate_bits):
        leaves = leaving >> q & 1
        here = jnp.where(leaves == 1, open_slots, closed_slots) & 15
        open_slots = open_slots >> 4 * leaves
        closed_slots = closed_slots >> 4 * (1 - leaves)
        slot.append(here)
        position_low = position_low + (here + gate_bits * leaves << 4 * q)
    for j in range(row_bits):
        position_high = position_high + (gate_bits + j - gate_bits * enters[j] << 4 * j)
    placed = []
    for b in range(nbits):
        low = position_low >> 4 * jnp.minimum(perm[b], gate_bits - 1) & 15
        high = position_high >> 4 * jnp.maximum(perm[b] - gate_bits, 0) & 15
        placed.append(jnp.where(perm[b] < gate_bits, low, high))

    def lane_map(places):
        return sum((lane >> k & 1) << place for k, place in enumerate(places))

    high_place = list(range(row_bits, gate_bits)) + [place - gate_bits for place in placed[gate_bits:]]
    maps = [lane_map(slot), lane_map(placed[:gate_bits]), lane_map(high_place)]
    return maps, enters


def split(x):
    high = x.astype(jnp.bfloat16)
    low = (x - high.astype(jnp.float32)).astype(jnp.bfloat16)
    return high, low


def dot(a, b, contract):
    return lax.dot_general(a, b, (contract, ((), ())), preferred_element_type=jnp.float32)


NT = ((1,), (1,))
NN = ((1,), (0,))


def swap_lane_bit(first, second, bit, lane, condition=None):
    width = first.shape[-1]
    axis = first.ndim - 1
    up = (lane >> bit & 1) == 1
    down = ~up
    if condition is not None:
        up = up & condition
        down = down & condition
    new_first = jnp.where(up, pltpu.roll(second, 1 << bit, axis), first)
    new_second = jnp.where(down, pltpu.roll(first, width - (1 << bit), axis), second)
    return new_first, new_second


def one_hot(lane_map):
    width = lane_map.shape[-1]
    rows = lax.broadcasted_iota(jnp.int32, (width, width), 0)
    return jnp.where(rows == lane_map, 1.0, 0.0).astype(jnp.bfloat16)


def stack_parts(real, imag):
    return jnp.concatenate([*split(real), *split(imag)])


def left_matrix(real, imag, columns):
    width = real.shape[-1]
    moved = dot(stack_parts(real, imag), columns, NT).astype(jnp.bfloat16)
    re_high, re_low, im_high, im_low = [moved[i * width : (i + 1) * width] for i in range(4)]

    def whole(re, im):
        return jnp.concatenate(
            [jnp.concatenate([re, -im], axis=1), jnp.concatenate([im, re], axis=1)], axis=0
        )

    return whole(re_high, im_high), whole(re_low, im_low)


def right_matrix(real, imag, columns):
    width = real.shape[-1]
    moved = dot(columns, stack_parts(real, imag), NT).astype(jnp.bfloat16)
    re_high, re_low, im_high, im_low = [moved[:, i * width : (i + 1) * width] for i in range(4)]

    def whole(re, im):
        return jnp.concatenate(
            [jnp.concatenate([re, im], axis=1), jnp.concatenate([-im, re], axis=1)], axis=0
        )

    return whole(re_high, im_high), whole(re_low, im_low)


def kernel(
    sizes,
    state_hbm,
    gates_hbm,
    perm_hbm,
    out_ref,
    state_ref,
    gates_ref,
    perm_ref,
    matrices,
    lanes_ref,
    swaps_ref,
    work,
    sent,
    landed,
    send_sem,
    recv_sem,
    load_sem,
):
    traj, nbits, gate_bits, dev_bits, halves = sizes
    width = 1 << gate_bits
    row_bits = nbits - gate_bits
    shared = gate_bits - row_bits
    per = 1 << shared
    rows = 1 << row_bits
    blocks = 1 << dev_bits
    top = blocks // 2
    wide = dev_bits > row_bits
    own_traj = traj // halves
    grp = lax.axis_index("grp")
    dev = lax.axis_index("dev")
    grp_low = grp % 2
    grp_next = grp // 2 % 2
    grp_rest = grp // 4 * 4
    dev_top = dev // top
    dev_low = dev % top


    def targets(cycle, step):
        low = (dev_low ^ (step % top)) if step % top else dev_low
        own = jnp.where(cycle == 0, grp_low, grp_next)
        high = 1 - own if step // top else own
        block = high * top + low
        to_grp = jnp.where(cycle == 0, grp_low * 2 + high, high * 2 + grp_low)
        to_dev = jnp.where(cycle == 0, grp_next, dev_top) * top + low
        slot = jnp.where(cycle == 0, dev_top, grp_next) * top + dev_low
        return block, grp_rest + to_grp, to_dev, slot

    stays = jnp.logical_and(grp_low == grp_next, grp_next == dev_top)

    barrier = pltpu.get_barrier_semaphore()
    for step in range(blocks):
        low = (dev_low ^ (step % top)) if step % top else dev_low
        high = step // top
        source_top = 1 - dev_top if high else dev_top
        first = (grp_rest + dev_top * 2 + grp_next, source_top * top + low)
        source_next = 1 - grp_next if high else grp_next
        second = (grp_rest + source_next * 2 + grp_low, dev_top * top + low)

        def tell(device):
            pl.semaphore_signal(barrier, inc=1, device_id=device, device_id_type=MESH)

        if step:
            tell(first)
            tell(second)
        else:
            pl.when(jnp.logical_not(stays))(functools.partial(tell, first))

    def gate_load(cycle, which):
        return pltpu.make_async_copy(
            gates_hbm.at[cycle, which], gates_ref.at[cycle, which], load_sem.at[2 + GATES * cycle + which]
        )

    perm_load = pltpu.make_async_copy(perm_hbm, perm_ref, load_sem.at[0])
    state_load = pltpu.make_async_copy(state_hbm, state_ref, load_sem.at[1])
    perm_load.start()
    state_load.start()
    for cycle in range(CYCLES):
        for which in range(GATES):
            gate_load(cycle, which).start()

    lane = lax.broadcasted_iota(jnp.int32, (1, width), 1)

    def keep_matrix(which, parts):
        matrices[which, 0] = parts[0]
        matrices[which, 1] = parts[1]

    def low_matrix(cycle, which, lane_map):
        gate_load(cycle, which).wait()
        parts = [gates_ref[cycle, which, part] for part in range(2)]
        keep_matrix(which, right_matrix(parts[0], parts[1], one_hot(lane_map)))

    def high_matrix(cycle, which, lane_map):
        gate_load(cycle, which).wait()
        parts = [
            jnp.concatenate(
                [gates_ref[cycle, which, part, pl.ds(a, rows, stride=per), :] for a in range(per)]
            )
            for part in range(2)
        ]
        keep_matrix(which, left_matrix(parts[0], parts[1], one_hot(lane_map)))


    def apply_low(planes, which):
        high, low = split(jnp.concatenate([jnp.concatenate(part) for part in planes], axis=1))
        m_high, m_low = matrices[which, 0], matrices[which, 1]
        y = dot(high, m_high, NN) + (dot(low, m_high, NN) + dot(high, m_low, NN))
        return [
            [y[t * rows : (t + 1) * rows, part * width : (part + 1) * width] for t in range(own_traj)]
            for part in range(2)
        ]

    def swap_traj(planes):
        planes = list(planes)
        for bit in range(shared):
            for t in range(len(planes)):
                if not t >> bit & 1:
                    o = t | 1 << bit
                    planes[t], planes[o] = swap_lane_bit(planes[t], planes[o], row_bits + bit, lane)
        return planes

    def apply_high(planes, which):
        operand = []
        for part in planes:
            part = swap_traj(part)
            operand.append(
                jnp.concatenate(
                    [jnp.concatenate(part[g : g + per]) for g in range(0, own_traj, per)], axis=1
                )
            )
        high, low = split(jnp.concatenate(operand))
        m_high, m_low = matrices[which, 0], matrices[which, 1]
        y = dot(m_high, high, NN) + (dot(m_low, high, NN) + dot(m_high, low, NN))
        return [
            swap_traj(
                [
                    y[part * width + a * rows : part * width + (a + 1) * rows, g * width : (g + 1) * width]
                    for g in range(own_traj // per)
                    for a in range(per)
                ]
            )
            for part in range(2)
        ]

    height = 2 * own_traj

    def local_part(half, cycle, conditions):
        x = jnp.concatenate(split(work[half]), axis=1)
        lanes = lanes_ref[...]
        y = dot(x, jnp.concatenate([lanes, lanes], axis=1), NT)
        tiles = [y[r * height : (r + 1) * height] for r in range(rows)]
        for j in range(row_bits):
            for r in range(rows):
                if not r >> j & 1:
                    o = r | 1 << j
                    tiles[r], tiles[o] = swap_lane_bit(tiles[r], tiles[o], j, lane, conditions[j])
        for r in range(rows):
            work[half, r * height : (r + 1) * height, :] = tiles[r]
        planes = [
            [work[half, pl.ds(part * own_traj + t, rows, stride=height), :] for t in range(own_traj)]
            for part in range(2)
        ]
        planes = apply_low(planes, 0)
        planes = apply_high(planes, 1)
        planes = apply_low(planes, 2)
        if wide:
            pairs = [swap_lane_bit(a, b, gate_bits - 1, lane) for a, b in zip(*planes)]
            planes = list(zip(*pairs))
        for part in range(2):
            for t in range(own_traj):
                sent[cycle, half, part, pl.ds(t, rows, stride=own_traj), :] = planes[part][t]

    def last_part(half, cycle):
        planes = [
            [landed[cycle, half, part, pl.ds(t, rows, stride=own_traj), :] for t in range(own_traj)]
            for part in range(2)
        ]
        if wide:
            pairs = [swap_lane_bit(a, b, gate_bits - 1, lane) for a, b in zip(*planes)]
            planes = list(zip(*pairs))
        planes = apply_high(planes, GATES - 1)
        for part in range(2):
            for t in range(own_traj):
                work[half, pl.ds(part * own_traj + t, rows, stride=height), :] = planes[part][t]

    def view(ref, cycle, half, block):
        if wide:
            start = pl.multiple_of(block // 2 * own_traj, own_traj)
            return ref.at[cycle, half, pl.ds(block % 2, 1), pl.ds(start, own_traj), :]
        depth = rows * own_traj // blocks
        start = pl.multiple_of(block * depth, depth)
        return ref.at[cycle, half, :, pl.ds(start, depth), :]

    def remote(cycle, half, step):
        block, to_grp, to_dev, slot = targets(cycle, step)
        return pltpu.make_async_remote_copy(
            src_ref=view(sent, cycle, half, block),
            dst_ref=view(landed, cycle, half, slot),
            send_sem=send_sem.at[cycle, half, step],
            recv_sem=recv_sem.at[cycle, half],
            device_id=(to_grp, to_dev),
            device_id_type=MESH,
        )

    def start(cycle, half):
        for step in range(blocks - 1, 0, -1):
            remote(cycle, half, step).start()

        def keep():
            block, _, _, slot = targets(cycle, 0)
            pltpu.make_async_copy(
                view(sent, cycle, half, block), view(landed, cycle, half, slot), recv_sem.at[cycle, half]
            ).start()

        own = jnp.logical_or(cycle == 1, stays)
        pl.when(own)(keep)
        pl.when(jnp.logical_not(own))(remote(cycle, half, 0).start)

    def finish(cycle, half):
        whole = landed.at[cycle, half]
        pltpu.make_async_copy(whole, whole, recv_sem.at[cycle, half]).wait()

    def finish_sends(cycle, half):
        for step in range(1, blocks):
            remote(cycle, half, step).wait_send()

        own = jnp.logical_or(cycle == 1, stays)
        pl.when(jnp.logical_not(own))(remote(cycle, half, 0).wait_send)

    perm_load.wait()
    state_load.wait()
    for half in range(halves):
        for r in range(rows):
            for part in range(2):
                start_row = r * height + part * own_traj
                work[half, start_row : start_row + own_traj, :] = state_ref[
                    part, half * own_traj : (half + 1) * own_traj, r * width : (r + 1) * width
                ]

    def stage(cycle, carry):
        @pl.when(cycle > 0)
        def _():
            high_matrix(cycle - 1, GATES - 1, (lane % per) * rows + lane // per)

        @pl.when(cycle < CYCLES)
        def _():
            perm = [perm_ref[cycle, b] for b in range(nbits)]
            maps, conditions = permutation_plan(perm, nbits, gate_bits, lane)
            lanes_ref[...] = one_hot(maps[0])
            for j in range(row_bits):
                swaps_ref[j] = conditions[j]
            low_matrix(cycle, 0, maps[1])
            high_matrix(cycle, 1, maps[2])
            low_matrix(cycle, 2, lane)

        def one_half(half, carry):
            @pl.when(cycle > 0)
            def _():
                finish(cycle - 1, half)
                last_part(half, cycle - 1)

            @pl.when(cycle < CYCLES)
            def _():
                local_part(half, cycle, [swaps_ref[j] == 1 for j in range(row_bits)])

                @pl.when(jnp.logical_and(cycle == 0, half == 0))
                def _():
                    pl.semaphore_wait(barrier, 2 * (blocks - 1) + jnp.where(stays, 0, 1))

                start(cycle, half)

            return carry

        return lax.fori_loop(0, halves, one_half, carry)

    lax.fori_loop(0, CYCLES + 1, stage, 0)
    for half in range(halves):
        for r in range(rows):
            for part in range(2):
                start_row = r * height + part * own_traj
                out_ref[
                    part, half * own_traj : (half + 1) * own_traj, r * width : (r + 1) * width
                ] = work[half, start_row : start_row + own_traj, :]

    def drain(index, carry):
        finish_sends(index // halves, index % halves)
        return carry

    lax.fori_loop(0, CYCLES * halves, drain, 0)


def on_device(state, gates, local_perm):
    traj = state.shape[1]
    nbits = state.shape[2].bit_length() - 1
    gate_bits = gates.shape[-1].bit_length() - 1
    dev_bits = lax.axis_size("dev").bit_length() - 1
    width = 1 << gate_bits
    rows = 1 << nbits - gate_bits
    halves = 2 if (rows * traj // 2 >> dev_bits) % 8 == 0 else 1
    sizes = (traj, nbits, gate_bits, dev_bits, halves)
    buffer = pltpu.VMEM((CYCLES, halves, 2, rows * traj // halves, width), jnp.float32)
    return pl.pallas_call(
        functools.partial(kernel, sizes),
        out_shape=jax.ShapeDtypeStruct(state.shape, state.dtype),
        in_specs=[pl.BlockSpec(memory_space=pltpu.HBM)] * 3,
        out_specs=pl.BlockSpec(memory_space=pltpu.VMEM),
        scratch_shapes=[
            pltpu.VMEM(state.shape, state.dtype),
            pltpu.VMEM(gates.shape, gates.dtype),
            pltpu.SMEM(local_perm.shape, local_perm.dtype),
            pltpu.VMEM((GATES, 2, 2 * width, 2 * width), jnp.bfloat16),
            pltpu.VMEM((width, width), jnp.bfloat16),
            pltpu.SMEM((nbits - gate_bits,), jnp.int32),
            pltpu.VMEM((halves, 2 * rows * traj // halves, width), jnp.float32),
            buffer,
            buffer,
            pltpu.SemaphoreType.DMA((CYCLES, halves, 1 << dev_bits)),
            pltpu.SemaphoreType.DMA((CYCLES, halves)),
            pltpu.SemaphoreType.DMA((2 + GATES * CYCLES,)),
        ],
        compiler_params=pltpu.CompilerParams(
            collective_id=0, has_side_effects=True, vmem_limit_bytes=32 << 20
        ),
    )(*[pltpu.with_memory_space_constraint(x, pltpu.HBM) for x in (state, gates, local_perm)])


def solution(mesh):
    placed = (P(None, None, ("grp", "dev")), P(), P())
    return jax.shard_map(
        on_device,
        mesh=mesh,
        in_specs=placed,
        out_specs=P(None, None, ("grp", "dev")),
        check_vma=False,
    )
```

```python
import functools

import jax
import jax.numpy as jnp
from jax import lax
from jax.experimental import pallas as pl
from jax.experimental.pallas import tpu as pltpu
from jax.sharding import PartitionSpec as P

MESH = pl.DeviceIdType.MESH
CYCLES = 2
GATES = 4


def permutation_plan(perm, nbits, gate_bits, lane):
    row_bits = nbits - gate_bits
    shared = gate_bits - row_bits
    leaving = sum(1 << perm[b] for b in range(gate_bits, nbits))
    enters = [1 - (leaving >> (gate_bits + j) & 1) for j in range(row_bits)]
    open_slots = closed_slots = 0
    open_at = closed_at = 0
    for j in range(gate_bits):
        is_open = enters[j] if j < row_bits else 0
        open_slots = open_slots + (j * is_open << open_at)
        closed_slots = closed_slots + (j * (1 - is_open) << closed_at)
        open_at = open_at + 4 * is_open
        closed_at = closed_at + 4 * (1 - is_open)
    slot = []
    position_low = position_high = 0
    for q in range(gate_bits):
        leaves = leaving >> q & 1
        here = jnp.where(leaves == 1, open_slots, closed_slots) & 15
        open_slots = open_slots >> 4 * leaves
        closed_slots = closed_slots >> 4 * (1 - leaves)
        slot.append(here)
        position_low = position_low + (here + gate_bits * leaves << 4 * q)
    for j in range(row_bits):
        position_high = position_high + (gate_bits + j - gate_bits * enters[j] << 4 * j)
    placed = []
    for b in range(nbits):
        low = position_low >> 4 * jnp.minimum(perm[b], gate_bits - 1) & 15
        high = position_high >> 4 * jnp.maximum(perm[b] - gate_bits, 0) & 15
        placed.append(jnp.where(perm[b] < gate_bits, low, high))

    def lane_map(places):
        return sum((lane >> k & 1) << place for k, place in enumerate(places))

    high_place = list(range(row_bits, gate_bits)) + [place - gate_bits for place in placed[gate_bits:]]
    maps = [lane_map(slot), lane_map(placed[:gate_bits]), lane_map(high_place)]
    return maps, [enter == 1 for enter in enters]


def split(x):
    high = x.astype(jnp.bfloat16)
    low = (x - high.astype(jnp.float32)).astype(jnp.bfloat16)
    return high, low


def dot(a, b, contract):
    return lax.dot_general(a, b, (contract, ((), ())), preferred_element_type=jnp.float32)


NT = ((1,), (1,))
NN = ((1,), (0,))


def swap_lane_bit(first, second, bit, lane, condition=None):
    width = first.shape[-1]
    axis = first.ndim - 1
    up = (lane >> bit & 1) == 1
    down = ~up
    if condition is not None:
        up = up & condition
        down = down & condition
    new_first = jnp.where(up, pltpu.roll(second, 1 << bit, axis), first)
    new_second = jnp.where(down, pltpu.roll(first, width - (1 << bit), axis), second)
    return new_first, new_second


def one_hot(lane_map):
    width = lane_map.shape[-1]
    rows = lax.broadcasted_iota(jnp.int32, (width, width), 0)
    return jnp.where(rows == lane_map, 1.0, 0.0).astype(jnp.bfloat16)


def stack_parts(real, imag):
    return jnp.concatenate([*split(real), *split(imag)])


def left_matrix(real, imag, columns):
    width = real.shape[-1]
    moved = dot(stack_parts(real, imag), columns, NT).astype(jnp.bfloat16)
    re_high, re_low, im_high, im_low = [moved[i * width : (i + 1) * width] for i in range(4)]

    def whole(re, im):
        return jnp.concatenate(
            [jnp.concatenate([re, -im], axis=1), jnp.concatenate([im, re], axis=1)], axis=0
        )

    return whole(re_high, im_high), whole(re_low, im_low)


def right_matrix(real, imag, columns):
    width = real.shape[-1]
    moved = dot(columns, stack_parts(real, imag), NT).astype(jnp.bfloat16)
    re_high, re_low, im_high, im_low = [moved[:, i * width : (i + 1) * width] for i in range(4)]

    def whole(re, im):
        return jnp.concatenate(
            [jnp.concatenate([re, im], axis=1), jnp.concatenate([-im, re], axis=1)], axis=0
        )

    return whole(re_high, im_high), whole(re_low, im_low)


def kernel(
    sizes,
    state_hbm,
    gates_hbm,
    perm_hbm,
    out_ref,
    state_ref,
    gates_ref,
    perm_ref,
    work,
    final,
    sent,
    landed,
    swapped,
    swap_sem,
    send_sem,
    recv_sem,
    load_sem,
):
    traj, nbits, gate_bits, dev_bits, halves = sizes
    width = 1 << gate_bits
    row_bits = nbits - gate_bits
    shared = gate_bits - row_bits
    per = 1 << shared
    rows = 1 << row_bits
    blocks = 1 << dev_bits
    top = blocks // 2
    wide = dev_bits > row_bits
    own_traj = traj // halves
    grp = lax.axis_index("grp")
    dev = lax.axis_index("dev")
    grp_low = grp % 2
    grp_next = grp // 2 % 2
    grp_rest = grp // 4 * 4
    dev_top = dev // top
    dev_low = dev % top


    def targets(cycle, step):
        low = (dev_low ^ (step % top)) if step % top else dev_low
        high = 1 - grp_next if step // top else grp_next
        block = high * top + low
        if cycle == 0:
            return block, grp, block, dev
        return block, grp_rest + high * 2 + grp_next, dev_top * top + low, grp_low * top + dev_low

    def stays(cycle, step):
        if step % top:
            return None
        if cycle == 0:
            return dev_top != grp_next if step else dev_top == grp_next
        return None if step else grp_low == grp_next

    other_grp = grp_rest + (1 - grp_next) * 2 + grp_low
    barrier = pltpu.get_barrier_semaphore()

    def tell(device):
        pl.semaphore_signal(barrier, inc=1, device_id=device, device_id_type=MESH)

    tell((other_grp, dev))
    for step in range(blocks):
        low = (dev_low ^ (step % top)) if step % top else dev_low
        if step:
            tell((grp, (1 - dev_top if step // top else dev_top) * top + low))
        source = (grp_rest + grp_low * 2 + (1 - grp_low if step // top else grp_low), dev_top * top + low)
        if step:
            tell(source)
        else:
            pl.when(grp_low != grp_next)(functools.partial(tell, source))

    loads = [
        pltpu.make_async_copy(perm_hbm, perm_ref, load_sem.at[0]),
        pltpu.make_async_copy(state_hbm, state_ref, load_sem.at[1]),
    ]
    for cycle in range(CYCLES):
        for which in range(GATES):
            sem = load_sem.at[2 + GATES * cycle + which]
            loads.append(
                pltpu.make_async_copy(gates_hbm.at[cycle, which], gates_ref.at[cycle, which], sem)
            )
    for load in loads:
        load.start()

    lane = lax.broadcasted_iota(jnp.int32, (1, width), 1)

    def low_matrix(cycle, which, lane_map):
        loads[2 + GATES * cycle + which].wait()
        return right_matrix(gates_ref[cycle, which, 0], gates_ref[cycle, which, 1], one_hot(lane_map))

    def high_matrix(cycle, which, lane_map):
        loads[2 + GATES * cycle + which].wait()
        parts = [
            jnp.concatenate(
                [gates_ref[cycle, which, part, pl.ds(a, rows, stride=per), :] for a in range(per)]
            )
            for part in range(2)
        ]
        return left_matrix(parts[0], parts[1], one_hot(lane_map))

    def plan_of(cycle):
        return permutation_plan([perm_ref[cycle, b] for b in range(nbits)], nbits, gate_bits, lane)

    def matrices_of(cycle, plan):
        maps, _ = plan
        return (
            low_matrix(cycle, 0, maps[1]),
            high_matrix(cycle, 1, maps[2]),
            low_matrix(cycle, 2, lane),
        )

    def last_matrix(cycle):
        return high_matrix(cycle, 3, (lane % per) * rows + lane // per)


    def apply_low(planes, matrix):
        high, low = split(jnp.concatenate([jnp.concatenate(part) for part in planes], axis=1))
        m_high, m_low = matrix
        y = dot(high, m_high, NN) + (dot(low, m_high, NN) + dot(high, m_low, NN))
        return [
            [y[t * rows : (t + 1) * rows, part * width : (part + 1) * width] for t in range(own_traj)]
            for part in range(2)
        ]

    def swap_traj(planes):
        planes = list(planes)
        for bit in range(shared):
            for t in range(len(planes)):
                if not t >> bit & 1:
                    o = t | 1 << bit
                    planes[t], planes[o] = swap_lane_bit(planes[t], planes[o], row_bits + bit, lane)
        return planes

    def apply_high(planes, matrix):
        operand = []
        for part in planes:
            part = swap_traj(part)
            operand.append(
                jnp.concatenate(
                    [jnp.concatenate(part[g : g + per]) for g in range(0, own_traj, per)], axis=1
                )
            )
        high, low = split(jnp.concatenate(operand))
        m_high, m_low = matrix
        y = dot(m_high, high, NN) + (dot(m_low, high, NN) + dot(m_high, low, NN))
        return [
            swap_traj(
                [
                    y[part * width + a * rows : part * width + (a + 1) * rows, g * width : (g + 1) * width]
                    for g in range(own_traj // per)
                    for a in range(per)
                ]
            )
            for part in range(2)
        ]

    def local_part(x, half, cycle, plan, matrices):
        maps, conditions = plan
        lanes = one_hot(maps[0])
        x = jnp.concatenate(split(x), axis=1)
        y = dot(x, jnp.concatenate([lanes, lanes], axis=1), NT)
        height = 2 * own_traj
        tiles = [y[r * height : (r + 1) * height] for r in range(rows)]
        for j in range(row_bits):
            for r in range(rows):
                if not r >> j & 1:
                    o = r | 1 << j
                    tiles[r], tiles[o] = swap_lane_bit(tiles[r], tiles[o], j, lane, conditions[j])
        for r in range(rows):
            work[half, r * height : (r + 1) * height, :] = tiles[r]
        planes = [
            [work[half, pl.ds(part * own_traj + t, rows, stride=height), :] for t in range(own_traj)]
            for part in range(2)
        ]
        planes = apply_low(planes, matrices[0])
        planes = apply_high(planes, matrices[1])
        planes = apply_low(planes, matrices[2])
        if wide:
            pairs = [swap_lane_bit(a, b, gate_bits - 1, lane) for a, b in zip(*planes)]
            planes = list(zip(*pairs))
        for part in range(2):
            for t in range(own_traj):
                sent[cycle, half, part, pl.ds(t, rows, stride=own_traj), :] = planes[part][t]

    def last_part(half, cycle, matrix):
        planes = [
            [landed[cycle, half, part, pl.ds(t, rows, stride=own_traj), :] for t in range(own_traj)]
            for part in range(2)
        ]
        if wide:
            pairs = [swap_lane_bit(a, b, gate_bits - 1, lane) for a, b in zip(*planes)]
            planes = list(zip(*pairs))
        return apply_high(planes, matrix)

    def view(ref, cycle, half, block):
        if wide:
            start = pl.multiple_of(block // 2 * own_traj, own_traj)
            return ref.at[cycle, half, pl.ds(block % 2, 1), pl.ds(start, own_traj), :]
        depth = rows * own_traj // blocks
        start = pl.multiple_of(block * depth, depth)
        return ref.at[cycle, half, :, pl.ds(start, depth), :]

    def source_of(cycle, half, step, block):
        if cycle == 0 and step // top:
            return view(swapped, 0, half, block % top)
        return view(sent, cycle, half, block)

    def swap(half):
        size = rows * own_traj // 2
        start = pl.multiple_of((1 - grp_next) * size, size)
        return pltpu.make_async_remote_copy(
            src_ref=sent.at[0, half, :, pl.ds(start, size), :],
            dst_ref=swapped.at[0, half],
            send_sem=swap_sem.at[0, half],
            recv_sem=swap_sem.at[1, half],
            device_id=(other_grp, dev),
            device_id_type=MESH,
        )

    def remote(cycle, half, step):
        block, to_grp, to_dev, slot = targets(cycle, step)
        return pltpu.make_async_remote_copy(
            src_ref=source_of(cycle, half, step, block),
            dst_ref=view(landed, cycle, half, slot),
            send_sem=send_sem.at[cycle, half, step],
            recv_sem=recv_sem.at[cycle, half],
            device_id=(to_grp, to_dev),
            device_id_type=MESH,
        )

    def start(cycle, half, steps):
        for step in reversed(steps):
            own = stays(cycle, step)
            if own is None:
                remote(cycle, half, step).start()
                continue

            def keep():
                block, _, _, slot = targets(cycle, step)
                pltpu.make_async_copy(
                    source_of(cycle, half, step, block),
                    view(landed, cycle, half, slot),
                    recv_sem.at[cycle, half],
                ).start()

            pl.when(own)(keep)
            pl.when(jnp.logical_not(own))(remote(cycle, half, step).start)

    def finish(cycle, half):
        whole = landed.at[cycle, half]
        pltpu.make_async_copy(whole, whole, recv_sem.at[cycle, half]).wait()

    def finish_sends(cycle, half):
        for step in range(blocks):
            own = stays(cycle, step)
            if own is None:
                remote(cycle, half, step).wait_send()
            else:
                pl.when(jnp.logical_not(own))(remote(cycle, half, step).wait_send)

    loads[0].wait()
    plan = plan_of(0)
    loads[1].wait()
    matrices = matrices_of(0, plan)
    for half in range(halves):
        tiles = []
        for r in range(rows):
            for part in range(2):
                tiles.append(
                    state_ref[
                        part, half * own_traj : (half + 1) * own_traj, r * width : (r + 1) * width
                    ]
                )
        local_part(jnp.concatenate(tiles), half, 0, plan, matrices)
        if half == 0:
            pl.semaphore_wait(barrier, 2 * blocks - 1 + jnp.where(grp_low == grp_next, 0, 1))
        swap(half).start()
        start(0, half, range(top))
    for half in range(halves):
        swap(half).wait_recv()
        start(0, half, range(top, blocks))
    last = last_matrix(0)
    plan = plan_of(1)
    matrices = matrices_of(1, plan)
    for half in range(halves):
        finish(0, half)
        planes = last_part(half, 0, last)
        height = 2 * own_traj
        for part in range(2):
            for t in range(own_traj):
                work[half, pl.ds(part * own_traj + t, rows, stride=height), :] = planes[part][t]
        local_part(work[half], half, 1, plan, matrices)
        start(1, half, range(blocks))
    last = last_matrix(1)
    for half in range(halves):
        finish(1, half)
        planes = last_part(half, 1, last)
        for part in range(2):
            for t in range(own_traj):
                final[part, pl.ds(half * own_traj + t, rows, stride=traj), :] = planes[part][t]
    for part in range(2):
        for r in range(rows):
            out_ref[part, :, r * width : (r + 1) * width] = final[part, r * traj : (r + 1) * traj, :]
    for half in range(halves):
        swap(half).wait_send()
    for cycle in range(CYCLES):
        for half in range(halves):
            finish_sends(cycle, half)


def on_device(state, gates, local_perm):
    traj = state.shape[1]
    nbits = state.shape[2].bit_length() - 1
    gate_bits = gates.shape[-1].bit_length() - 1
    dev_bits = lax.axis_size("dev").bit_length() - 1
    width = 1 << gate_bits
    rows = 1 << nbits - gate_bits
    halves = 2 if (rows * traj // 2 >> dev_bits) % 8 == 0 else 1
    sizes = (traj, nbits, gate_bits, dev_bits, halves)
    buffer = pltpu.VMEM((CYCLES, halves, 2, rows * traj // halves, width), jnp.float32)
    return pl.pallas_call(
        functools.partial(kernel, sizes),
        out_shape=jax.ShapeDtypeStruct(state.shape, state.dtype),
        in_specs=[pl.BlockSpec(memory_space=pltpu.HBM)] * 3,
        out_specs=pl.BlockSpec(memory_space=pltpu.VMEM),
        scratch_shapes=[
            pltpu.VMEM(state.shape, state.dtype),
            pltpu.VMEM(gates.shape, gates.dtype),
            pltpu.SMEM(local_perm.shape, local_perm.dtype),
            pltpu.VMEM((halves, 2 * rows * traj // halves, width), jnp.float32),
            pltpu.VMEM((2, rows * traj, width), jnp.float32),
            buffer,
            buffer,
            pltpu.VMEM((1, halves, 2, rows * traj // halves // 2, width), jnp.float32),
            pltpu.SemaphoreType.DMA((2, halves)),
            pltpu.SemaphoreType.DMA((CYCLES, halves, 1 << dev_bits)),
            pltpu.SemaphoreType.DMA((CYCLES, halves)),
            pltpu.SemaphoreType.DMA((2 + GATES * CYCLES,)),
        ],
        compiler_params=pltpu.CompilerParams(
            collective_id=0, has_side_effects=True, vmem_limit_bytes=32 << 20
        ),
    )(*[pltpu.with_memory_space_constraint(x, pltpu.HBM) for x in (state, gates, local_perm)])


def solution(mesh):
    placed = (P(None, None, ("grp", "dev")), P(), P())
    return jax.shard_map(
        on_device,
        mesh=mesh,
        in_specs=placed,
        out_specs=P(None, None, ("grp", "dev")),
        check_vma=False,
    )
```

```python
import functools

import jax
import jax.numpy as jnp
from jax import lax
from jax.experimental import pallas as pl
from jax.experimental.pallas import tpu as pltpu
from jax.sharding import PartitionSpec as P

MESH = pl.DeviceIdType.MESH
CYCLES = 2
GATES = 4


def permutation_plan(perm, nbits, gate_bits, lane):
    row_bits = nbits - gate_bits
    shared = gate_bits - row_bits
    leaving = sum(1 << perm[b] for b in range(gate_bits, nbits))
    enters = [1 - (leaving >> (gate_bits + j) & 1) for j in range(row_bits)]
    open_slots = closed_slots = 0
    open_at = closed_at = 0
    for j in range(gate_bits):
        is_open = enters[j] if j < row_bits else 0
        open_slots = open_slots + (j * is_open << open_at)
        closed_slots = closed_slots + (j * (1 - is_open) << closed_at)
        open_at = open_at + 4 * is_open
        closed_at = closed_at + 4 * (1 - is_open)
    slot = []
    position_low = position_high = 0
    for q in range(gate_bits):
        leaves = leaving >> q & 1
        here = jnp.where(leaves == 1, open_slots, closed_slots) & 15
        open_slots = open_slots >> 4 * leaves
        closed_slots = closed_slots >> 4 * (1 - leaves)
        slot.append(here)
        position_low = position_low + (here + gate_bits * leaves << 4 * q)
    for j in range(row_bits):
        position_high = position_high + (gate_bits + j - gate_bits * enters[j] << 4 * j)
    placed = []
    for b in range(nbits):
        low = position_low >> 4 * jnp.minimum(perm[b], gate_bits - 1) & 15
        high = position_high >> 4 * jnp.maximum(perm[b] - gate_bits, 0) & 15
        placed.append(jnp.where(perm[b] < gate_bits, low, high))

    def lane_map(places):
        return sum((lane >> k & 1) << place for k, place in enumerate(places))

    high_place = list(range(row_bits, gate_bits)) + [place - gate_bits for place in placed[gate_bits:]]
    maps = [lane_map(slot), lane_map(placed[:gate_bits]), lane_map(high_place)]
    return maps, [enter == 1 for enter in enters]


def split(x):
    high = x.astype(jnp.bfloat16)
    low = (x - high.astype(jnp.float32)).astype(jnp.bfloat16)
    return high, low


def dot(a, b, contract):
    return lax.dot_general(a, b, (contract, ((), ())), preferred_element_type=jnp.float32)


NT = ((1,), (1,))
NN = ((1,), (0,))


def swap_lane_bit(first, second, bit, lane, condition=None):
    width = first.shape[-1]
    axis = first.ndim - 1
    up = (lane >> bit & 1) == 1
    down = ~up
    if condition is not None:
        up = up & condition
        down = down & condition
    new_first = jnp.where(up, pltpu.roll(second, 1 << bit, axis), first)
    new_second = jnp.where(down, pltpu.roll(first, width - (1 << bit), axis), second)
    return new_first, new_second


def one_hot(lane_map):
    width = lane_map.shape[-1]
    rows = lax.broadcasted_iota(jnp.int32, (width, width), 0)
    return jnp.where(rows == lane_map, 1.0, 0.0).astype(jnp.bfloat16)


def stack_parts(real, imag):
    return jnp.concatenate([*split(real), *split(imag)])


def left_matrix(real, imag, columns):
    width = real.shape[-1]
    moved = dot(stack_parts(real, imag), columns, NT).astype(jnp.bfloat16)
    re_high, re_low, im_high, im_low = [moved[i * width : (i + 1) * width] for i in range(4)]

    def whole(re, im):
        return jnp.concatenate(
            [jnp.concatenate([re, -im], axis=1), jnp.concatenate([im, re], axis=1)], axis=0
        )

    high, low = whole(re_high, im_high), whole(re_low, im_low)
    return jnp.concatenate([high, low, high], axis=1)


def right_matrix(real, imag, columns):
    width = real.shape[-1]
    moved = dot(columns, stack_parts(real, imag), NT).astype(jnp.bfloat16)
    re_high, re_low, im_high, im_low = [moved[:, i * width : (i + 1) * width] for i in range(4)]

    def whole(re, im):
        return jnp.concatenate(
            [jnp.concatenate([re, im], axis=1), jnp.concatenate([-im, re], axis=1)], axis=0
        )

    high, low = whole(re_high, im_high), whole(re_low, im_low)
    return jnp.concatenate([high, low, high], axis=0)


def kernel(
    sizes,
    state_hbm,
    gates_hbm,
    perm_hbm,
    out_ref,
    state_ref,
    gates_ref,
    perm_ref,
    work,
    final,
    sent,
    landed,
    swapped,
    swap_sem,
    send_sem,
    recv_sem,
    load_sem,
):
    traj, nbits, gate_bits, dev_bits, halves = sizes
    width = 1 << gate_bits
    row_bits = nbits - gate_bits
    shared = gate_bits - row_bits
    per = 1 << shared
    rows = 1 << row_bits
    blocks = 1 << dev_bits
    top = blocks // 2
    wide = dev_bits > row_bits
    own_traj = traj // halves
    grp = lax.axis_index("grp")
    dev = lax.axis_index("dev")
    grp_low = grp % 2
    grp_next = grp // 2 % 2
    grp_rest = grp // 4 * 4
    dev_top = dev // top
    dev_low = dev % top


    def targets(cycle, step):
        low = (dev_low ^ (step % top)) if step % top else dev_low
        high = 1 - grp_next if step // top else grp_next
        block = high * top + low
        if cycle == 0:
            return block, grp, block, dev
        return block, grp_rest + high * 2 + grp_next, dev_top * top + low, grp_low * top + dev_low

    def stays(cycle, step):
        if step % top:
            return None
        if cycle == 0:
            return dev_top != grp_next if step else dev_top == grp_next
        return None if step else grp_low == grp_next

    loads = [
        pltpu.make_async_copy(perm_hbm, perm_ref, load_sem.at[0]),
        pltpu.make_async_copy(state_hbm, state_ref, load_sem.at[1]),
    ]
    for cycle in range(CYCLES):
        for which in range(GATES):
            sem = load_sem.at[2 + GATES * cycle + which]
            loads.append(
                pltpu.make_async_copy(gates_hbm.at[cycle, which], gates_ref.at[cycle, which], sem)
            )
    for load in loads:
        load.start()

    other_grp = grp_rest + (1 - grp_next) * 2 + grp_low
    barrier = pltpu.get_barrier_semaphore()

    def tell(device):
        pl.semaphore_signal(barrier, inc=1, device_id=device, device_id_type=MESH)

    tell((other_grp, dev))
    for step in range(blocks):
        low = (dev_low ^ (step % top)) if step % top else dev_low
        if step:
            tell((grp, (1 - dev_top if step // top else dev_top) * top + low))
        source = (grp_rest + grp_low * 2 + (1 - grp_low if step // top else grp_low), dev_top * top + low)
        if step:
            tell(source)
        else:
            pl.when(grp_low != grp_next)(functools.partial(tell, source))

    lane = lax.broadcasted_iota(jnp.int32, (1, width), 1)

    def low_matrix(cycle, which, lane_map):
        loads[2 + GATES * cycle + which].wait()
        return right_matrix(gates_ref[cycle, which, 0], gates_ref[cycle, which, 1], one_hot(lane_map))

    def high_matrix(cycle, which, lane_map):
        loads[2 + GATES * cycle + which].wait()
        parts = [
            jnp.concatenate(
                [gates_ref[cycle, which, part, pl.ds(a, rows, stride=per), :] for a in range(per)]
            )
            for part in range(2)
        ]
        return left_matrix(parts[0], parts[1], one_hot(lane_map))

    def plan_of(cycle):
        return permutation_plan([perm_ref[cycle, b] for b in range(nbits)], nbits, gate_bits, lane)

    def matrices_of(cycle, plan):
        maps, _ = plan
        return (
            low_matrix(cycle, 0, maps[1]),
            high_matrix(cycle, 1, maps[2]),
            low_matrix(cycle, 2, lane),
        )

    def last_matrix(cycle):
        return high_matrix(cycle, 3, (lane % per) * rows + lane // per)


    def apply_low(planes, matrix):
        high, low = split(jnp.concatenate([jnp.concatenate(part) for part in planes], axis=1))
        y = dot(jnp.concatenate([high, high, low], axis=1), matrix, NN)
        return [
            [y[t * rows : (t + 1) * rows, part * width : (part + 1) * width] for t in range(own_traj)]
            for part in range(2)
        ]

    def swap_traj(planes):
        planes = list(planes)
        for bit in range(shared):
            for t in range(len(planes)):
                if not t >> bit & 1:
                    o = t | 1 << bit
                    planes[t], planes[o] = swap_lane_bit(planes[t], planes[o], row_bits + bit, lane)
        return planes

    def apply_high(planes, matrix):
        operand = []
        for part in planes:
            part = swap_traj(part)
            operand.append(
                jnp.concatenate(
                    [jnp.concatenate(part[g : g + per]) for g in range(0, own_traj, per)], axis=1
                )
            )
        high, low = split(jnp.concatenate(operand))
        y = dot(matrix, jnp.concatenate([high, high, low]), NN)
        return [
            swap_traj(
                [
                    y[part * width + a * rows : part * width + (a + 1) * rows, g * width : (g + 1) * width]
                    for g in range(own_traj // per)
                    for a in range(per)
                ]
            )
            for part in range(2)
        ]

    def local_part(x, half, cycle, plan, matrices):
        maps, conditions = plan
        lanes = one_hot(maps[0])
        x = jnp.concatenate(split(x), axis=1)
        y = dot(x, jnp.concatenate([lanes, lanes], axis=1), NT)
        height = 2 * own_traj
        tiles = [y[r * height : (r + 1) * height] for r in range(rows)]
        for j in range(row_bits):
            for r in range(rows):
                if not r >> j & 1:
                    o = r | 1 << j
                    tiles[r], tiles[o] = swap_lane_bit(tiles[r], tiles[o], j, lane, conditions[j])
        for r in range(rows):
            work[half, r * height : (r + 1) * height, :] = tiles[r]
        planes = [
            [work[half, pl.ds(part * own_traj + t, rows, stride=height), :] for t in range(own_traj)]
            for part in range(2)
        ]
        planes = apply_low(planes, matrices[0])
        planes = apply_high(planes, matrices[1])
        planes = apply_low(planes, matrices[2])
        if wide:
            pairs = [swap_lane_bit(a, b, gate_bits - 1, lane) for a, b in zip(*planes)]
            planes = list(zip(*pairs))
        for part in range(2):
            for t in range(own_traj):
                sent[cycle, half, part, pl.ds(t, rows, stride=own_traj), :] = planes[part][t]

    def last_part(half, cycle, matrix):
        planes = [
            [landed[cycle, half, part, pl.ds(t, rows, stride=own_traj), :] for t in range(own_traj)]
            for part in range(2)
        ]
        if wide:
            pairs = [swap_lane_bit(a, b, gate_bits - 1, lane) for a, b in zip(*planes)]
            planes = list(zip(*pairs))
        return apply_high(planes, matrix)

    def view(ref, cycle, half, block):
        if wide:
            start = pl.multiple_of(block // 2 * own_traj, own_traj)
            return ref.at[cycle, half, pl.ds(block % 2, 1), pl.ds(start, own_traj), :]
        depth = rows * own_traj // blocks
        start = pl.multiple_of(block * depth, depth)
        return ref.at[cycle, half, :, pl.ds(start, depth), :]

    def source_of(cycle, half, step, block):
        if cycle == 0 and step // top:
            return view(swapped, 0, half, block % top)
        return view(sent, cycle, half, block)

    def swap(half):
        size = rows * own_traj // 2
        start = pl.multiple_of((1 - grp_next) * size, size)
        return pltpu.make_async_remote_copy(
            src_ref=sent.at[0, half, :, pl.ds(start, size), :],
            dst_ref=swapped.at[0, half],
            send_sem=swap_sem.at[0, half],
            recv_sem=swap_sem.at[1, half],
            device_id=(other_grp, dev),
            device_id_type=MESH,
        )

    def remote(cycle, half, step):
        block, to_grp, to_dev, slot = targets(cycle, step)
        return pltpu.make_async_remote_copy(
            src_ref=source_of(cycle, half, step, block),
            dst_ref=view(landed, cycle, half, slot),
            send_sem=send_sem.at[cycle, half, step],
            recv_sem=recv_sem.at[cycle, half],
            device_id=(to_grp, to_dev),
            device_id_type=MESH,
        )

    def start(cycle, half, steps):
        for step in reversed(steps):
            own = stays(cycle, step)
            if own is None:
                remote(cycle, half, step).start()
                continue

            def keep():
                block, _, _, slot = targets(cycle, step)
                pltpu.make_async_copy(
                    source_of(cycle, half, step, block),
                    view(landed, cycle, half, slot),
                    recv_sem.at[cycle, half],
                ).start()

            pl.when(own)(keep)
            pl.when(jnp.logical_not(own))(remote(cycle, half, step).start)

    def finish(cycle, half):
        whole = landed.at[cycle, half]
        pltpu.make_async_copy(whole, whole, recv_sem.at[cycle, half]).wait()

    def finish_sends(cycle, half):
        for step in range(blocks):
            own = stays(cycle, step)
            if own is None:
                remote(cycle, half, step).wait_send()
            else:
                pl.when(jnp.logical_not(own))(remote(cycle, half, step).wait_send)

    loads[0].wait()
    plan = plan_of(0)
    loads[1].wait()
    matrices = matrices_of(0, plan)
    for half in range(halves):
        tiles = []
        for r in range(rows):
            for part in range(2):
                tiles.append(
                    state_ref[
                        part, half * own_traj : (half + 1) * own_traj, r * width : (r + 1) * width
                    ]
                )
        local_part(jnp.concatenate(tiles), half, 0, plan, matrices)
        if half == 0:
            pl.semaphore_wait(barrier, 2 * blocks - 1 + jnp.where(grp_low == grp_next, 0, 1))
        swap(half).start()
        start(0, half, range(top))
    for half in range(halves):
        swap(half).wait_recv()
        start(0, half, range(top, blocks))
    last = last_matrix(0)
    plan = plan_of(1)
    matrices = matrices_of(1, plan)
    for half in range(halves):
        finish(0, half)
        planes = last_part(half, 0, last)
        height = 2 * own_traj
        for part in range(2):
            for t in range(own_traj):
                work[half, pl.ds(part * own_traj + t, rows, stride=height), :] = planes[part][t]
        local_part(work[half], half, 1, plan, matrices)
        start(1, half, range(blocks))
    last = last_matrix(1)
    for half in range(halves):
        finish(1, half)
        planes = last_part(half, 1, last)
        for part in range(2):
            for t in range(own_traj):
                final[part, pl.ds(half * own_traj + t, rows, stride=traj), :] = planes[part][t]
    for part in range(2):
        for r in range(rows):
            out_ref[part, :, r * width : (r + 1) * width] = final[part, r * traj : (r + 1) * traj, :]
    for half in range(halves):
        swap(half).wait_send()
    for cycle in range(CYCLES):
        for half in range(halves):
            finish_sends(cycle, half)


def on_device(state, gates, local_perm):
    traj = state.shape[1]
    nbits = state.shape[2].bit_length() - 1
    gate_bits = gates.shape[-1].bit_length() - 1
    dev_bits = lax.axis_size("dev").bit_length() - 1
    width = 1 << gate_bits
    rows = 1 << nbits - gate_bits
    halves = 2 if (rows * traj // 2 >> dev_bits) % 8 == 0 else 1
    sizes = (traj, nbits, gate_bits, dev_bits, halves)
    buffer = pltpu.VMEM((CYCLES, halves, 2, rows * traj // halves, width), jnp.float32)
    return pl.pallas_call(
        functools.partial(kernel, sizes),
        out_shape=jax.ShapeDtypeStruct(state.shape, state.dtype),
        in_specs=[pl.BlockSpec(memory_space=pltpu.HBM)] * 3,
        out_specs=pl.BlockSpec(memory_space=pltpu.VMEM),
        scratch_shapes=[
            pltpu.VMEM(state.shape, state.dtype),
            pltpu.VMEM(gates.shape, gates.dtype),
            pltpu.SMEM(local_perm.shape, local_perm.dtype),
            pltpu.VMEM((halves, 2 * rows * traj // halves, width), jnp.float32),
            pltpu.VMEM((2, rows * traj, width), jnp.float32),
            buffer,
            buffer,
            pltpu.VMEM((1, halves, 2, rows * traj // halves // 2, width), jnp.float32),
            pltpu.SemaphoreType.DMA((2, halves)),
            pltpu.SemaphoreType.DMA((CYCLES, halves, 1 << dev_bits)),
            pltpu.SemaphoreType.DMA((CYCLES, halves)),
            pltpu.SemaphoreType.DMA((2 + GATES * CYCLES,)),
        ],
        compiler_params=pltpu.CompilerParams(
            collective_id=0, has_side_effects=True, vmem_limit_bytes=32 << 20
        ),
    )(*[pltpu.with_memory_space_constraint(x, pltpu.HBM) for x in (state, gates, local_perm)])


def solution(mesh):
    placed = (P(None, None, ("grp", "dev")), P(), P())
    return jax.shard_map(
        on_device,
        mesh=mesh,
        in_specs=placed,
        out_specs=P(None, None, ("grp", "dev")),
        check_vma=False,
    )
```

```python
import functools

import jax
import jax.numpy as jnp
from jax import lax
from jax.experimental import pallas as pl
from jax.experimental.pallas import tpu as pltpu
from jax.sharding import PartitionSpec as P

MESH = pl.DeviceIdType.MESH
CYCLES = 2
GATES = 4


def permutation_plan(perm, nbits, gate_bits, lane):
    row_bits = nbits - gate_bits
    shared = gate_bits - row_bits
    leaving = sum(1 << perm[b] for b in range(gate_bits, nbits))
    enters = [1 - (leaving >> (gate_bits + j) & 1) for j in range(row_bits)]
    open_slots = closed_slots = 0
    open_at = closed_at = 0
    for j in range(gate_bits):
        is_open = enters[j] if j < row_bits else 0
        open_slots = open_slots + (j * is_open << open_at)
        closed_slots = closed_slots + (j * (1 - is_open) << closed_at)
        open_at = open_at + 4 * is_open
        closed_at = closed_at + 4 * (1 - is_open)
    slot = []
    position_low = position_high = 0
    for q in range(gate_bits):
        leaves = leaving >> q & 1
        here = jnp.where(leaves == 1, open_slots, closed_slots) & 15
        open_slots = open_slots >> 4 * leaves
        closed_slots = closed_slots >> 4 * (1 - leaves)
        slot.append(here)
        position_low = position_low + (here + gate_bits * leaves << 4 * q)
    for j in range(row_bits):
        position_high = position_high + (gate_bits + j - gate_bits * enters[j] << 4 * j)
    placed = []
    for b in range(nbits):
        low = position_low >> 4 * jnp.minimum(perm[b], gate_bits - 1) & 15
        high = position_high >> 4 * jnp.maximum(perm[b] - gate_bits, 0) & 15
        placed.append(jnp.where(perm[b] < gate_bits, low, high))

    def lane_map(places):
        return sum((lane >> k & 1) << place for k, place in enumerate(places))

    high_place = list(range(row_bits, gate_bits)) + [place - gate_bits for place in placed[gate_bits:]]
    maps = [lane_map(slot), lane_map(placed[:gate_bits]), lane_map(high_place)]
    return maps, [enter == 1 for enter in enters]


def split(x):
    high = x.astype(jnp.bfloat16)
    low = (x - high.astype(jnp.float32)).astype(jnp.bfloat16)
    return high, low


def dot(a, b, contract):
    return lax.dot_general(a, b, (contract, ((), ())), preferred_element_type=jnp.float32)


NT = ((1,), (1,))
NN = ((1,), (0,))


def swap_lane_bit(first, second, bit, lane, condition=None):
    width = first.shape[-1]
    axis = first.ndim - 1
    up = (lane >> bit & 1) == 1
    down = ~up
    if condition is not None:
        up = up & condition
        down = down & condition
    new_first = jnp.where(up, pltpu.roll(second, 1 << bit, axis), first)
    new_second = jnp.where(down, pltpu.roll(first, width - (1 << bit), axis), second)
    return new_first, new_second


def one_hot(lane_map):
    width = lane_map.shape[-1]
    rows = lax.broadcasted_iota(jnp.int32, (width, width), 0)
    return jnp.where(rows == lane_map, 1.0, 0.0).astype(jnp.bfloat16)


def stack_parts(real, imag):
    return jnp.concatenate([*split(real), *split(imag)])


def left_matrix(real, imag, columns):
    width = real.shape[-1]
    moved = dot(stack_parts(real, imag), columns, NT).astype(jnp.bfloat16)
    re_high, re_low, im_high, im_low = [moved[i * width : (i + 1) * width] for i in range(4)]

    def whole(re, im):
        return jnp.concatenate(
            [jnp.concatenate([re, -im], axis=1), jnp.concatenate([im, re], axis=1)], axis=0
        )

    high, low = whole(re_high, im_high), whole(re_low, im_low)
    return jnp.concatenate([high, low, high], axis=1)


def right_matrix(real, imag, columns):
    width = real.shape[-1]
    moved = dot(columns, stack_parts(real, imag), NT).astype(jnp.bfloat16)
    re_high, re_low, im_high, im_low = [moved[:, i * width : (i + 1) * width] for i in range(4)]

    def whole(re, im):
        return jnp.concatenate(
            [jnp.concatenate([re, im], axis=1), jnp.concatenate([-im, re], axis=1)], axis=0
        )

    high, low = whole(re_high, im_high), whole(re_low, im_low)
    return jnp.concatenate([high, low, high], axis=0)


def kernel(
    sizes,
    state_hbm,
    gates_hbm,
    perm_hbm,
    out_ref,
    state_ref,
    gates_ref,
    perm_ref,
    work,
    final,
    sent,
    landed,
    swapped,
    swap_sem,
    send_sem,
    recv_sem,
    load_sem,
):
    traj, nbits, gate_bits, dev_bits, halves = sizes
    width = 1 << gate_bits
    row_bits = nbits - gate_bits
    shared = gate_bits - row_bits
    per = 1 << shared
    rows = 1 << row_bits
    blocks = 1 << dev_bits
    top = blocks // 2
    wide = dev_bits > row_bits
    own_traj = traj // halves
    grp = lax.axis_index("grp")
    dev = lax.axis_index("dev")
    grp_low = grp % 2
    grp_next = grp // 2 % 2
    grp_rest = grp // 4 * 4
    dev_top = dev // top
    dev_low = dev % top


    def targets(cycle, step):
        low = (dev_low ^ (step % top)) if step % top else dev_low
        high = 1 - grp_next if step // top else grp_next
        block = high * top + low
        if cycle == 0:
            return block, grp, block, dev
        return block, grp_rest + high * 2 + grp_next, dev_top * top + low, grp_low * top + dev_low

    def stays(cycle, step):
        if step % top:
            return None
        if cycle == 0:
            return dev_top != grp_next if step else dev_top == grp_next
        return None if step else grp_low == grp_next

    loads = [
        pltpu.make_async_copy(perm_hbm, perm_ref, load_sem.at[0]),
        pltpu.make_async_copy(state_hbm, state_ref, load_sem.at[1]),
    ]
    for cycle in range(CYCLES):
        for which in range(GATES):
            sem = load_sem.at[2 + GATES * cycle + which]
            loads.append(
                pltpu.make_async_copy(gates_hbm.at[cycle, which], gates_ref.at[cycle, which], sem)
            )
    for load in loads:
        load.start()

    other_grp = grp_rest + (1 - grp_next) * 2 + grp_low
    barrier = pltpu.get_barrier_semaphore()

    def tell(device):
        pl.semaphore_signal(barrier, inc=1, device_id=device, device_id_type=MESH)

    tell((other_grp, dev))
    for step in range(blocks):
        low = (dev_low ^ (step % top)) if step % top else dev_low
        if step:
            tell((grp, (1 - dev_top if step // top else dev_top) * top + low))
        source = (grp_rest + grp_low * 2 + (1 - grp_low if step // top else grp_low), dev_top * top + low)
        if step:
            tell(source)
        else:
            pl.when(grp_low != grp_next)(functools.partial(tell, source))

    lane = lax.broadcasted_iota(jnp.int32, (1, width), 1)

    def low_matrix(cycle, which, lane_map):
        loads[2 + GATES * cycle + which].wait()
        return right_matrix(gates_ref[cycle, which, 0], gates_ref[cycle, which, 1], one_hot(lane_map))

    def high_matrix(cycle, which, lane_map):
        loads[2 + GATES * cycle + which].wait()
        parts = [
            jnp.concatenate(
                [gates_ref[cycle, which, part, pl.ds(a, rows, stride=per), :] for a in range(per)]
            )
            for part in range(2)
        ]
        return left_matrix(parts[0], parts[1], one_hot(lane_map))

    def plan_of(cycle):
        return permutation_plan([perm_ref[cycle, b] for b in range(nbits)], nbits, gate_bits, lane)

    def matrices_of(cycle, plan):
        maps, _ = plan
        return (
            low_matrix(cycle, 0, maps[1]),
            high_matrix(cycle, 1, maps[2]),
            low_matrix(cycle, 2, lane),
        )

    def last_matrix(cycle):
        return high_matrix(cycle, 3, (lane % per) * rows + lane // per)


    def apply_low(planes, matrix):
        high, low = split(jnp.concatenate([jnp.concatenate(part) for part in planes], axis=1))
        y = dot(jnp.concatenate([high, high, low], axis=1), matrix, NN)
        return [
            [y[t * rows : (t + 1) * rows, part * width : (part + 1) * width] for t in range(own_traj)]
            for part in range(2)
        ]

    def swap_traj(planes):
        planes = list(planes)
        for bit in range(shared):
            for t in range(len(planes)):
                if not t >> bit & 1:
                    o = t | 1 << bit
                    planes[t], planes[o] = swap_lane_bit(planes[t], planes[o], row_bits + bit, lane)
        return planes

    def apply_high(planes, matrix):
        operand = []
        for part in planes:
            part = swap_traj(part)
            operand.append(
                jnp.concatenate(
                    [jnp.concatenate(part[g : g + per]) for g in range(0, own_traj, per)], axis=1
                )
            )
        high, low = split(jnp.concatenate(operand))
        y = dot(matrix, jnp.concatenate([high, high, low]), NN)
        return [
            swap_traj(
                [
                    y[part * width + a * rows : part * width + (a + 1) * rows, g * width : (g + 1) * width]
                    for g in range(own_traj // per)
                    for a in range(per)
                ]
            )
            for part in range(2)
        ]

    def local_part(x, half, cycle, plan, matrices):
        maps, conditions = plan
        lanes = one_hot(maps[0])
        x = jnp.concatenate(split(x), axis=1)
        y = dot(x, jnp.concatenate([lanes, lanes], axis=1), NT)
        height = 2 * own_traj
        tiles = [y[r * height : (r + 1) * height] for r in range(rows)]
        for j in range(row_bits):
            for r in range(rows):
                if not r >> j & 1:
                    o = r | 1 << j
                    tiles[r], tiles[o] = swap_lane_bit(tiles[r], tiles[o], j, lane, conditions[j])
        for r in range(rows):
            work[half, r * height : (r + 1) * height, :] = tiles[r]
        planes = [
            [work[half, pl.ds(part * own_traj + t, rows, stride=height), :] for t in range(own_traj)]
            for part in range(2)
        ]
        planes = apply_low(planes, matrices[0])
        planes = apply_high(planes, matrices[1])
        planes = apply_low(planes, matrices[2])
        if wide:
            pairs = [swap_lane_bit(a, b, gate_bits - 1, lane) for a, b in zip(*planes)]
            planes = list(zip(*pairs))
        for part in range(2):
            for t in range(own_traj):
                sent[cycle, half, part, pl.ds(t, rows, stride=own_traj), :] = planes[part][t]

    def last_part(half, cycle, matrix):
        planes = [
            [landed[cycle, half, part, pl.ds(t, rows, stride=own_traj), :] for t in range(own_traj)]
            for part in range(2)
        ]
        if wide:
            pairs = [swap_lane_bit(a, b, gate_bits - 1, lane) for a, b in zip(*planes)]
            planes = list(zip(*pairs))
        return apply_high(planes, matrix)

    def view(ref, cycle, half, block):
        if wide:
            start = pl.multiple_of(block // 2 * own_traj, own_traj)
            return ref.at[cycle, half, pl.ds(block % 2, 1), pl.ds(start, own_traj), :]
        depth = rows * own_traj // blocks
        start = pl.multiple_of(block * depth, depth)
        return ref.at[cycle, half, :, pl.ds(start, depth), :]

    def source_of(cycle, half, step, block):
        if cycle == 0 and step // top:
            return view(swapped, 0, half, block % top)
        return view(sent, cycle, half, block)

    def swap(half, step):
        low = (dev_low ^ step) if step else dev_low
        return pltpu.make_async_remote_copy(
            src_ref=view(sent, 0, half, (1 - grp_next) * top + low),
            dst_ref=view(swapped, 0, half, low),
            send_sem=swap_sem.at[0, half, step],
            recv_sem=swap_sem.at[1, half, step],
            device_id=(other_grp, dev),
            device_id_type=MESH,
        )

    def remote(cycle, half, step):
        block, to_grp, to_dev, slot = targets(cycle, step)
        return pltpu.make_async_remote_copy(
            src_ref=source_of(cycle, half, step, block),
            dst_ref=view(landed, cycle, half, slot),
            send_sem=send_sem.at[cycle, half, step],
            recv_sem=recv_sem.at[cycle, half],
            device_id=(to_grp, to_dev),
            device_id_type=MESH,
        )

    def start(cycle, half, steps):
        for step in reversed(steps):
            own = stays(cycle, step)
            if own is None:
                remote(cycle, half, step).start()
                continue

            def keep():
                block, _, _, slot = targets(cycle, step)
                pltpu.make_async_copy(
                    source_of(cycle, half, step, block),
                    view(landed, cycle, half, slot),
                    recv_sem.at[cycle, half],
                ).start()

            pl.when(own)(keep)
            pl.when(jnp.logical_not(own))(remote(cycle, half, step).start)

    def finish(cycle, half):
        whole = landed.at[cycle, half]
        pltpu.make_async_copy(whole, whole, recv_sem.at[cycle, half]).wait()

    def finish_sends(cycle, half):
        for step in range(blocks):
            own = stays(cycle, step)
            if own is None:
                remote(cycle, half, step).wait_send()
            else:
                pl.when(jnp.logical_not(own))(remote(cycle, half, step).wait_send)

    loads[0].wait()
    plan = plan_of(0)
    loads[1].wait()
    matrices = matrices_of(0, plan)
    for half in range(halves):
        tiles = []
        for r in range(rows):
            for part in range(2):
                tiles.append(
                    state_ref[
                        part, half * own_traj : (half + 1) * own_traj, r * width : (r + 1) * width
                    ]
                )
        local_part(jnp.concatenate(tiles), half, 0, plan, matrices)
        if half == 0:
            pl.semaphore_wait(barrier, 2 * blocks - 1 + jnp.where(grp_low == grp_next, 0, 1))
        for step in reversed(range(top)):
            swap(half, step).start()
        start(0, half, range(top))
    for half in range(halves):
        for step in reversed(range(top)):
            swap(half, step).wait_recv()
            start(0, half, [top + step])
    last = last_matrix(0)
    plan = plan_of(1)
    matrices = matrices_of(1, plan)
    for half in range(halves):
        finish(0, half)
        planes = last_part(half, 0, last)
        height = 2 * own_traj
        for part in range(2):
            for t in range(own_traj):
                work[half, pl.ds(part * own_traj + t, rows, stride=height), :] = planes[part][t]
        local_part(work[half], half, 1, plan, matrices)
        start(1, half, range(blocks))
    last = last_matrix(1)
    for half in range(halves):
        finish(1, half)
        planes = last_part(half, 1, last)
        for part in range(2):
            for t in range(own_traj):
                final[part, pl.ds(half * own_traj + t, rows, stride=traj), :] = planes[part][t]
    for part in range(2):
        for r in range(rows):
            out_ref[part, :, r * width : (r + 1) * width] = final[part, r * traj : (r + 1) * traj, :]
    for half in range(halves):
        for step in range(top):
            swap(half, step).wait_send()
    for cycle in range(CYCLES):
        for half in range(halves):
            finish_sends(cycle, half)


def on_device(state, gates, local_perm):
    traj = state.shape[1]
    nbits = state.shape[2].bit_length() - 1
    gate_bits = gates.shape[-1].bit_length() - 1
    dev_bits = lax.axis_size("dev").bit_length() - 1
    width = 1 << gate_bits
    rows = 1 << nbits - gate_bits
    halves = 2 if (rows * traj // 2 >> dev_bits) % 8 == 0 else 1
    sizes = (traj, nbits, gate_bits, dev_bits, halves)
    buffer = pltpu.VMEM((CYCLES, halves, 2, rows * traj // halves, width), jnp.float32)
    return pl.pallas_call(
        functools.partial(kernel, sizes),
        out_shape=jax.ShapeDtypeStruct(state.shape, state.dtype),
        in_specs=[pl.BlockSpec(memory_space=pltpu.HBM)] * 3,
        out_specs=pl.BlockSpec(memory_space=pltpu.VMEM),
        scratch_shapes=[
            pltpu.VMEM(state.shape, state.dtype),
            pltpu.VMEM(gates.shape, gates.dtype),
            pltpu.SMEM(local_perm.shape, local_perm.dtype),
            pltpu.VMEM((halves, 2 * rows * traj // halves, width), jnp.float32),
            pltpu.VMEM((2, rows * traj, width), jnp.float32),
            buffer,
            buffer,
            pltpu.VMEM((1, halves, 2, rows * traj // halves // 2, width), jnp.float32),
            pltpu.SemaphoreType.DMA((2, halves, 1 << dev_bits - 1)),
            pltpu.SemaphoreType.DMA((CYCLES, halves, 1 << dev_bits)),
            pltpu.SemaphoreType.DMA((CYCLES, halves)),
            pltpu.SemaphoreType.DMA((2 + GATES * CYCLES,)),
        ],
        compiler_params=pltpu.CompilerParams(
            collective_id=0, has_side_effects=True, vmem_limit_bytes=32 << 20
        ),
    )(*[pltpu.with_memory_space_constraint(x, pltpu.HBM) for x in (state, gates, local_perm)])


def solution(mesh):
    placed = (P(None, None, ("grp", "dev")), P(), P())
    return jax.shard_map(
        on_device,
        mesh=mesh,
        in_specs=placed,
        out_specs=P(None, None, ("grp", "dev")),
        check_vma=False,
    )
```
